32 devices in a mesh: grp: 2 (over x), gy: 4 (over y, core), gz: 4 (over z).
Axes of the slice: x: 2, y: 2, z: 4, core: 2. Of those that a mesh axis runs over, the one named last changes fastest.
Arguments:
- velocity: float32 [3, 32, 32, 256], P(None, 'gy', 'gz', 'grp'), may hold values from -5 to 5
- basis_old: bfloat16 [64, 3, 16, 16, 256], P(None, None, 'gy', 'gz', 'grp'), may hold values from -64 to 64
- strength: float32 [64], replicated, may hold values from 0.3 to 3
- snapshots: bfloat16 [63, 3, 16, 16, 256], P(None, None, 'gy', 'gz', 'grp'), may hold values from -64 to 64
Outputs:
- advanced: float32 [3, 32, 32, 256], P(None, 'gy', 'gz', 'grp')
- basis_new: bfloat16 [128, 3, 16, 16, 256], P(None, None, 'gy', 'gz', 'grp')
- root_factor: float32 [128, 128], replicated
The draws below stay inside these ranges and needn't reach their ends.
All inputs are finite; a program needn't handle non-finite values.
Results may differ from the reference program's by a relative error of at most 0.0012.
The reference program's roundings to bfloat16 on the way (of `newest`, `head`, `whole` and `weights`) count: a program that leaves them out, or rounds other values in their place, can miss the bound.
Values sent between devices are 32-bit elements; how exact they have to be, the bound alone decides.
A program may use at most 64 MiB of HBM per device.

```python
import math
import jax
import jax.numpy as jnp
from jax import lax

MODES = 64
BATCH = 63
NS_ITERS = 8
NX = 256
NY = 32
NZ = 32
RANKS = 128
MROWS = 196608


def shared_fields(key):
    return jax.random.normal(jax.random.fold_in(key, 9001), (4, 3, NY // 2, NZ // 2, NX), jnp.float32)


def mixed_rows(key, row_count, salt_value):
    fields = shared_fields(key)
    salted = jax.random.fold_in(key, salt_value)
    leading = jax.random.uniform(jax.random.fold_in(salted, 1), (row_count, 1), jnp.float32, 0.5, 1.0)
    others = 0.5 * jax.random.normal(jax.random.fold_in(salted, 2), (row_count, 3), jnp.float32)
    coeffs = jnp.concatenate([leading, others], axis=1)
    fluctuation = jax.random.normal(jax.random.fold_in(salted, 3), (row_count, 3, NY // 2, NZ // 2, NX), jnp.float32)
    return jnp.einsum('rk,kcyzx->rcyzx', coeffs, fields) + fluctuation


def scaled_rows(key, row_count, salt_value):
    rows = mixed_rows(key, row_count, salt_value)
    return jnp.clip(rows, -64.0, 64.0).astype(jnp.bfloat16)


def draw_basis_old(key, part):
    return scaled_rows(key, MODES, 11)


def draw_snapshots(key, part):
    return scaled_rows(key, BATCH, 21)


def draw_velocity(key, part):
    leading = shared_fields(key)[0]
    magnitude = jax.random.uniform(jax.random.fold_in(key, 31), (3, NY, NZ, NX), jnp.float32, 2.0, 5.0)
    coin = jax.random.uniform(jax.random.fold_in(key, 32), (3, NY, NZ, NX), jnp.float32)
    signed = jnp.where(coin < 0.5, -magnitude, magnitude)
    placed = jnp.zeros((3, NY, NZ, NX), jnp.float32).at[:, ::2, ::2, :].set(0.6 * leading)
    return jnp.clip(signed + placed, -5.0, 5.0)


def setup_inputs(seed: int = 0) -> dict:
    streams_of = jax.random.split(jax.random.key(seed), 5)
    velocity = draw_velocity(jax.random.fold_in(streams_of[4], 71), 0)
    basis_old = draw_basis_old(jax.random.fold_in(streams_of[4], 71), 0)
    strength = jnp.clip(jnp.exp(jax.random.uniform(streams_of[2], (MODES,), jnp.float32, math.log(0.3), math.log(3.0))), 0.3, 3.0)
    snapshots = draw_snapshots(jax.random.fold_in(streams_of[4], 71), 0)
    return {"velocity": velocity, "basis_old": basis_old, "strength": strength, "snapshots": snapshots}


time_step = 0.1
viscosity = 0.05

def padding(field):
    wrapped = jnp.pad(field, ((0, 0), (0, 0), (1, 1), (1, 1)), mode='wrap')
    return jnp.pad(wrapped, ((0, 0), (1, 1), (0, 0), (0, 0)))

def tendency(padded, field):
    y_plus = padded[:, 2:, 1:-1, 1:-1]
    y_minus = padded[:, :-2, 1:-1, 1:-1]
    z_plus = padded[:, 1:-1, 2:, 1:-1]
    z_minus = padded[:, 1:-1, :-2, 1:-1]
    x_plus = padded[:, 1:-1, 1:-1, 2:]
    x_minus = padded[:, 1:-1, 1:-1, :-2]
    carried = field[0][None] * (x_plus - x_minus) * 0.5
    carried = carried + field[1][None] * (y_plus - y_minus) * 0.5
    carried = carried + field[2][None] * (z_plus - z_minus) * 0.5
    spread = x_plus + x_minus + y_plus + y_minus + z_plus + z_minus - 6.0 * field
    return viscosity * spread - carried

def reference(velocity, basis_old, strength, snapshots):
    field = velocity
    for repeat in range(2):
        first = field + time_step * tendency(padding(field), field)
        second = 0.75 * field + 0.25 * (first + time_step * tendency(padding(first), first))
        field = field / 3.0 + 2.0 / 3.0 * (second + time_step * tendency(padding(second), second))
    newest = field[:, ::2, ::2, :].reshape(1, -1).astype(jnp.bfloat16)
    head = (strength[:, None] * basis_old.reshape(MODES, -1).astype(jnp.float32)).astype(jnp.bfloat16)
    whole = jnp.concatenate([head, snapshots.reshape(BATCH, -1), newest], axis=0)
    gram = jnp.dot(whole, whole.T, preferred_element_type=jnp.float32)
    scale = jnp.sqrt(jnp.sum(gram * gram))
    level = gram / scale
    ident = jnp.eye(RANKS, dtype=jnp.float32)
    inverse = ident
    for repeat in range(NS_ITERS):
        factor = 1.5 * ident - 0.5 * jnp.dot(inverse, level, precision=lax.Precision.HIGHEST)
        level = jnp.dot(level, factor, precision=lax.Precision.HIGHEST)
        inverse = jnp.dot(factor, inverse, precision=lax.Precision.HIGHEST)
    weights = (inverse * (jnp.sqrt(jnp.float32(MROWS)) / jnp.sqrt(scale))).astype(jnp.bfloat16)
    block_count = 3 * (NY // 2)
    whole_blocks = whole.reshape(RANKS, block_count, -1)

    def rotate(block_index):
        block = lax.dynamic_index_in_dim(whole_blocks, block_index, 1, keepdims=False)
        return jnp.dot(weights, block, preferred_element_type=jnp.float32).astype(jnp.bfloat16)
    pieces = lax.map(rotate, jnp.arange(block_count, dtype=jnp.int32))
    basis_new = jnp.transpose(pieces, (1, 0, 2)).reshape(RANKS, 3, NY // 2, NZ // 2, NX)
    return (field, basis_new, level)
```

```python
import functools

import jax
import jax.numpy as jnp
from jax import lax
from jax.experimental import pallas as pl
from jax.experimental.pallas import tpu as pltpu
from jax.sharding import PartitionSpec as P

NS_ITERS = 8
STAGES = 6
MESH = pl.DeviceIdType.MESH

time_step = 0.1
viscosity = 0.05


def each(count, body):
    if count <= 8:
        for i in range(count):
            body(i)
    else:
        lax.fori_loop(0, count, lambda i, carry: (body(i), carry)[1], 0)


def kernel(
    sizes, rows_total, v_ref, earlier_ref,
    field_ref, level_ref, basis_ref,
    stage, zsend, xsend, yrecv, zrecv, xrecv,
    gram_ref, part_ref, plane_ref, line_ref, full_ref,
    cross_send, cross_plane, cross_mid, cross_line,
    ysend_sem, yrecv_sem, zsend_sem, zrecv_sem, xsend_sem, xrecv_sem,
    asend_sem, arecv_sem, bsend_sem, brecv_sem, csend_sem, crecv_sem,
    dsend_sem, drecv_sem, esend_sem, erecv_sem,
):
    n_grp, n_gy, n_gz = sizes
    grp, gy, gz = lax.axis_index("grp"), lax.axis_index("gy"), lax.axis_index("gz")
    n_plane = n_grp * n_gy
    me = grp * n_gy + gy
    comps, ny, nz, nx = v_ref.shape
    ranks = earlier_ref.shape[0]
    lines = comps * ny

    def plane_id(offset):
        peer = lax.rem(me + offset, n_plane)
        return peer, {"grp": peer // n_gy, "gy": lax.rem(peer, n_gy)}

    def line_id(offset):
        peer = lax.rem(gz + offset, n_gz)
        return peer, {"gz": peer}

    y_up, y_down = {"gy": lax.rem(gy + 1, n_gy)}, {"gy": lax.rem(gy + n_gy - 1, n_gy)}
    z_up, z_down = {"gz": lax.rem(gz + 1, n_gz)}, {"gz": lax.rem(gz + n_gz - 1, n_gz)}
    x_up, x_down = {"grp": lax.rem(grp + 1, n_grp)}, {"grp": lax.rem(grp + n_grp - 1, n_grp)}
    x_ways = 1 if n_grp == 2 else 2

    barrier = pltpu.get_barrier_semaphore()

    def greet_plane(i):
        pl.semaphore_signal(barrier, inc=1, device_id=plane_id(i + 1)[1], device_id_type=MESH)

    def greet_line(i):
        pl.semaphore_signal(barrier, inc=1, device_id=line_id(i + 1)[1], device_id_type=MESH)

    each(n_plane - 1, greet_plane)
    each(n_gz - 1, greet_line)
    pl.semaphore_wait(barrier, n_plane + n_gz - 2)

    def remote(src, dst, send_sem, recv_sem, target):
        return pltpu.make_async_remote_copy(
            src_ref=src, dst_ref=dst, send_sem=send_sem, recv_sem=recv_sem,
            device_id=target, device_id_type=MESH,
        )

    def halo_copies(s):
        copies = [
            remote(stage.at[s, :, ny - 1], yrecv.at[s, 0], ysend_sem.at[s, 0], yrecv_sem.at[s, 0], y_up),
            remote(stage.at[s, :, 0], yrecv.at[s, 1], ysend_sem.at[s, 1], yrecv_sem.at[s, 1], y_down),
            remote(zsend.at[s, 0], zrecv.at[s, 0], zsend_sem.at[s, 0], zrecv_sem.at[s, 0], z_up),
            remote(zsend.at[s, 1], zrecv.at[s, 1], zsend_sem.at[s, 1], zrecv_sem.at[s, 1], z_down),
            remote(xsend.at[s], xrecv.at[s, 0], xsend_sem.at[s, 0], xrecv_sem.at[s, 0], x_up),
        ]
        if x_ways == 2:
            copies.append(
                remote(xsend.at[s], xrecv.at[s, 1], xsend_sem.at[s, 1], xrecv_sem.at[s, 1], x_down)
            )
        return copies

    lane = lax.broadcasted_iota(jnp.int32, (lines, nz, nx), 2)
    line = lax.broadcasted_iota(jnp.int32, (lines, nz, nx), 0)
    row = lax.broadcasted_iota(jnp.int32, (lines, nz, nx), 1)
    low_lane = lane == line
    high_lane = lane == line + nx // 2

    def send(s, f):
        stage[s] = f
        zsend[s, 0] = f[:, :, nz - 1, :]
        zsend[s, 1] = f[:, :, 0, :]
        flat = f.reshape(lines, nz, nx)
        packed = jnp.where(low_lane, flat[:, :, 0:1], 0.0)
        packed = packed + jnp.where(high_lane, flat[:, :, nx - 1 : nx], 0.0)
        xsend[s] = jnp.sum(packed, axis=0)
        copies = halo_copies(s)
        for copy in copies:
            copy.start()
        return copies

    def stepped(s, f, copies):
        for copy in copies:
            copy.wait_recv()
        flat = f.reshape(lines, nz, nx)
        bottom = jnp.where(gy == 0, 0.0, yrecv[s, 0])
        upper = jnp.where(gy == n_gy - 1, 0.0, yrecv[s, 1])
        y_minus = jnp.concatenate([bottom[:, None], f[:, :-1]], axis=1)
        y_plus = jnp.concatenate([f[:, 1:], upper[:, None]], axis=1)
        z_low = zrecv[s, 0].reshape(lines, 1, nx)
        z_high = zrecv[s, 1].reshape(lines, 1, nx)
        z_minus = jnp.where(row == 0, z_low, pltpu.roll(flat, 1, 1)).reshape(f.shape)
        z_plus = jnp.where(row == nz - 1, z_high, pltpu.roll(flat, nz - 1, 1)).reshape(f.shape)
        from_left, from_right = xrecv[s, 0], xrecv[s, x_ways - 1]
        x_low = jnp.sum(jnp.where(high_lane, from_left[None], 0.0), axis=2, keepdims=True)
        x_high = jnp.sum(jnp.where(low_lane, from_right[None], 0.0), axis=2, keepdims=True)
        x_minus = jnp.where(lane == 0, x_low, pltpu.roll(flat, 1, 2)).reshape(f.shape)
        x_plus = jnp.where(lane == nx - 1, x_high, pltpu.roll(flat, nx - 1, 2)).reshape(f.shape)
        carried = f[0][None] * (x_plus - x_minus) * 0.5
        carried = carried + f[1][None] * (y_plus - y_minus) * 0.5
        carried = carried + f[2][None] * (z_plus - z_minus) * 0.5
        spread = x_plus + x_minus + y_plus + y_minus + z_plus + z_minus - 6.0 * f
        return f + time_step * (viscosity * spread - carried)

    def scatter_copy(i):
        peer, target = plane_id(i + 1)
        return remote(
            gram_ref.at[peer], plane_ref.at[me], asend_sem.at[i], arecv_sem.at[me], target
        )

    def line_copy(i):
        _, target = line_id(i + 1)
        return remote(part_ref, line_ref.at[gz], bsend_sem.at[i], brecv_sem.at[gz], target)

    def gather_copy(i):
        _, target = plane_id(i + 1)
        return remote(
            full_ref.at[me], full_ref.at[me], csend_sem.at[i], crecv_sem.at[me], target
        )

    def cross_plane_copy(i):
        _, target = plane_id(i + 1)
        return remote(cross_send, cross_plane.at[me], dsend_sem.at[i], drecv_sem.at[me], target)

    def cross_line_copy(i):
        _, target = line_id(i + 1)
        return remote(cross_mid, cross_line.at[gz], esend_sem.at[i], erecv_sem.at[gz], target)

    def wait_plane(buffer, sem):
        def body(i):
            peer, target = plane_id(i + 1)
            remote(buffer.at[peer], buffer.at[peer], sem.at[peer], sem.at[peer], target).wait_recv()

        each(n_plane - 1, body)

    def wait_line(buffer, sem):
        def body(i):
            peer, target = line_id(i + 1)
            remote(buffer.at[peer], buffer.at[peer], sem.at[peer], sem.at[peer], target).wait_recv()

        each(n_gz - 1, body)

    def begin_gram():
        earlier = earlier_ref[...]
        gram = lax.dot_general(
            earlier, earlier, (((1,), (1,)), ((), ())), preferred_element_type=jnp.float32
        )
        gram_ref[...] = gram.reshape(gram_ref.shape)
        plane_ref[me] = gram_ref[me]
        each(n_plane - 1, lambda i: scatter_copy(i).start())

    def add_plane():
        wait_plane(plane_ref, arecv_sem)
        part = jnp.sum(plane_ref[...], axis=0)
        part_ref[...] = part
        line_ref[gz] = part
        each(n_gz - 1, lambda i: line_copy(i).start())

    def add_line():
        wait_line(line_ref, brecv_sem)
        full_ref[me] = jnp.sum(line_ref[...], axis=0)
        each(n_plane - 1, lambda i: gather_copy(i).start())

    between = {0: begin_gram, 2: add_plane, 3: add_line}
    base = v_ref[...]
    f = base
    for s in range(STAGES):
        copies = send(s, f)
        if s in between:
            between[s]()
        moved = stepped(s, f, copies)
        if s % 3 == 0:
            f = moved
        elif s % 3 == 1:
            f = 0.75 * base + 0.25 * moved
        else:
            f = base / 3.0 + 2.0 / 3.0 * moved
            base = f
    field_ref[...] = f

    blocks = [(c, y, z) for c in range(comps) for y in range(0, ny, 2) for z in range(0, nz, 2)]

    def newest_block(b):
        c, y, z = blocks[b]
        return field_ref[c, y, pl.ds(z, 1), :].astype(jnp.bfloat16).astype(jnp.float32)

    total = jnp.zeros((ranks, nx), jnp.float32)
    own = jnp.zeros((1, nx), jnp.float32)
    for b in range(len(blocks)):
        newest = newest_block(b)
        total = total + earlier_ref[:, b * nx : (b + 1) * nx].astype(jnp.float32) * newest
        own = own + newest * newest
    square_row = lax.broadcasted_iota(jnp.int32, (ranks, ranks), 0)
    square_col = lax.broadcasted_iota(jnp.int32, (ranks, ranks), 1)
    total = jnp.where(lax.broadcasted_iota(jnp.int32, (ranks, nx), 0) == ranks - 1, own, total)
    cross = jnp.sum(total.T, axis=0, keepdims=True)
    cross_send[...] = jnp.broadcast_to(cross, cross_send.shape)
    cross_plane[me] = cross_send[...]
    each(n_plane - 1, lambda i: cross_plane_copy(i).start())
    wait_plane(full_ref, crecv_sem)
    wait_plane(cross_plane, drecv_sem)
    cross_mid[...] = jnp.sum(cross_plane[...], axis=0)
    cross_line[gz] = cross_mid[...]
    each(n_gz - 1, lambda i: cross_line_copy(i).start())
    wait_line(cross_line, erecv_sem)
    cross = jnp.sum(cross_line[...], axis=0)[0:1]
    cross = jnp.broadcast_to(cross, (ranks, ranks))

    gram = full_ref[...].reshape(ranks, ranks)
    gram = jnp.where(square_col == ranks - 1, cross.T, gram)
    gram = jnp.where(square_row == ranks - 1, cross, gram)
    scale = jnp.sqrt(jnp.sum(gram * gram, keepdims=True))
    level = gram / scale
    ident = jnp.where(square_row == square_col, 1.0, 0.0)
    dot = functools.partial(
        jnp.dot, precision=lax.Precision.HIGHEST, preferred_element_type=jnp.float32
    )
    inverse = ident
    for repeat in range(NS_ITERS):
        product = level if repeat == 0 else dot(inverse, level)
        factor = 1.5 * ident - 0.5 * product
        level = dot(level, factor)
        inverse = factor if repeat == 0 else dot(factor, inverse)
    level_ref[...] = level
    factor = jnp.sqrt(jnp.full((1, 1), rows_total, jnp.float32)) / jnp.sqrt(scale)
    weights = (inverse * factor).astype(jnp.bfloat16)
    last = lax.broadcasted_iota(jnp.int32, (ranks, nx), 0) == ranks - 1
    for b in range(len(blocks)):
        block = earlier_ref[:, b * nx : (b + 1) * nx].astype(jnp.float32)
        block = jnp.where(last, newest_block(b), block).astype(jnp.bfloat16)
        basis_ref[:, b * nx : (b + 1) * nx] = jnp.dot(
            weights, block, preferred_element_type=jnp.float32
        ).astype(jnp.bfloat16)

    for s in range(STAGES):
        for copy in halo_copies(s):
            copy.wait_send()
    each(n_plane - 1, lambda i: scatter_copy(i).wait_send())
    each(n_gz - 1, lambda i: line_copy(i).wait_send())
    each(n_plane - 1, lambda i: gather_copy(i).wait_send())
    each(n_plane - 1, lambda i: cross_plane_copy(i).wait_send())
    each(n_gz - 1, lambda i: cross_line_copy(i).wait_send())


def local(velocity, basis_old, strength, snapshots):
    modes = basis_old.shape[0]
    earlier_count = snapshots.shape[0]
    ranks = modes + earlier_count + 1
    sizes = tuple(lax.axis_size(axis) for axis in ("grp", "gy", "gz"))
    n_grp, n_gy, n_gz = sizes
    n_plane = n_grp * n_gy
    comps, ny, nz, nx = velocity.shape
    head = (strength[:, None] * basis_old.reshape(modes, -1).astype(jnp.float32)).astype(
        jnp.bfloat16
    )
    length = head.shape[1]
    earlier = jnp.concatenate(
        [head, snapshots.reshape(earlier_count, -1), jnp.zeros((1, length), jnp.bfloat16)], axis=0
    )
    share = ranks // n_plane
    assert share * n_plane == ranks
    f32 = jnp.float32
    dma = pltpu.SemaphoreType.DMA
    vmem = pl.BlockSpec(memory_space=pltpu.VMEM)
    field, level, basis_new = pl.pallas_call(
        functools.partial(kernel, sizes, float(length * n_plane * n_gz)),
        out_shape=(
            jax.ShapeDtypeStruct(velocity.shape, f32),
            jax.ShapeDtypeStruct((ranks, ranks), f32),
            jax.ShapeDtypeStruct((ranks, length), jnp.bfloat16),
        ),
        in_specs=[vmem, vmem],
        out_specs=(vmem, vmem, vmem),
        scratch_shapes=[
            pltpu.VMEM((STAGES,) + velocity.shape, f32),
            pltpu.VMEM((STAGES, 2, comps, ny, nx), f32),
            pltpu.VMEM((STAGES, nz, nx), f32),
            pltpu.VMEM((STAGES, 2, comps, nz, nx), f32),
            pltpu.VMEM((STAGES, 2, comps, ny, nx), f32),
            pltpu.VMEM((STAGES, 2, nz, nx), f32),
            pltpu.VMEM((n_plane, share, ranks), f32),
            pltpu.VMEM((share, ranks), f32),
            pltpu.VMEM((n_plane, share, ranks), f32),
            pltpu.VMEM((n_gz, share, ranks), f32),
            pltpu.VMEM((n_plane, share, ranks), f32),
            pltpu.VMEM((8, ranks), f32),
            pltpu.VMEM((n_plane, 8, ranks), f32),
            pltpu.VMEM((8, ranks), f32),
            pltpu.VMEM((n_gz, 8, ranks), f32),
            dma((STAGES, 2)), dma((STAGES, 2)),
            dma((STAGES, 2)), dma((STAGES, 2)),
            dma((STAGES, 2)), dma((STAGES, 2)),
            dma((n_plane,)), dma((n_plane,)),
            dma((n_gz,)), dma((n_gz,)),
            dma((n_plane,)), dma((n_plane,)),
            dma((n_plane,)), dma((n_plane,)),
            dma((n_gz,)), dma((n_gz,)),
        ],
        compiler_params=pltpu.CompilerParams(
            collective_id=0, has_side_effects=True, vmem_limit_bytes=24 * 1024 * 1024
        ),
    )(velocity, earlier)
    basis_new = basis_new.reshape(ranks, comps, ny // 2, nz // 2, nx)
    return (field, basis_new, level)


def solution(mesh):
    placed = (
        P(None, "gy", "gz", "grp"),
        P(None, None, "gy", "gz", "grp"),
        P(),
        P(None, None, "gy", "gz", "grp"),
    )
    return jax.shard_map(
        local,
        mesh=mesh,
        in_specs=placed,
        out_specs=(P(None, "gy", "gz", "grp"), P(None, None, "gy", "gz", "grp"), P()),
        check_vma=False,
    )
```

```python
import functools

import jax
import jax.numpy as jnp
from jax import lax
from jax.experimental import pallas as pl
from jax.experimental.pallas import tpu as pltpu
from jax.sharding import PartitionSpec as P

NS_ITERS = 8
STAGES = 6
MESH = pl.DeviceIdType.MESH

time_step = 0.1
viscosity = 0.05


def each(count, body):
    if count <= 8:
        for i in range(count):
            body(i)
    else:
        lax.fori_loop(0, count, lambda i, carry: (body(i), carry)[1], 0)


def kernel(
    sizes, rows_total, v_ref, strength_ref, old_hbm, snap_hbm,
    field_ref, level_ref, weights_ref, earlier_ref,
    old_ref, snap_ref, wide_ref, load_sem,
    stage, zsend, xsend, yrecv, zrecv, xrecv,
    gram_ref, part_ref, plane_ref, line_ref, full_ref,
    cross_send, cross_plane, cross_mid, cross_line,
    ysend_sem, yrecv_sem, zsend_sem, zrecv_sem, xsend_sem, xrecv_sem,
    asend_sem, arecv_sem, bsend_sem, brecv_sem, csend_sem, crecv_sem,
    dsend_sem, drecv_sem, esend_sem, erecv_sem,
):
    n_grp, n_gy, n_gz = sizes
    grp, gy, gz = lax.axis_index("grp"), lax.axis_index("gy"), lax.axis_index("gz")
    n_plane = n_grp * n_gy
    me = grp * n_gy + gy
    comps, ny, nz, nx = v_ref.shape
    ranks = earlier_ref.shape[0]
    lines = comps * ny

    def plane_id(offset):
        peer = lax.rem(me + offset, n_plane)
        return peer, {"grp": peer // n_gy, "gy": lax.rem(peer, n_gy)}

    def line_id(offset):
        peer = lax.rem(gz + offset, n_gz)
        return peer, {"gz": peer}

    y_up, y_down = {"gy": lax.rem(gy + 1, n_gy)}, {"gy": lax.rem(gy + n_gy - 1, n_gy)}
    z_up, z_down = {"gz": lax.rem(gz + 1, n_gz)}, {"gz": lax.rem(gz + n_gz - 1, n_gz)}
    x_up, x_down = {"grp": lax.rem(grp + 1, n_grp)}, {"grp": lax.rem(grp + n_grp - 1, n_grp)}
    x_ways = 1 if n_grp == 2 else 2

    loads = [
        pltpu.make_async_copy(old_hbm, old_ref, load_sem.at[0]),
        pltpu.make_async_copy(snap_hbm, snap_ref, load_sem.at[1]),
    ]
    for load in loads:
        load.start()
    barrier = pltpu.get_barrier_semaphore()

    def greet_plane(i):
        pl.semaphore_signal(barrier, inc=1, device_id=plane_id(i + 1)[1], device_id_type=MESH)

    def greet_line(i):
        pl.semaphore_signal(barrier, inc=1, device_id=line_id(i + 1)[1], device_id_type=MESH)

    each(n_plane - 1, greet_plane)
    each(n_gz - 1, greet_line)
    pl.semaphore_wait(barrier, n_plane + n_gz - 2)

    def remote(src, dst, send_sem, recv_sem, target):
        return pltpu.make_async_remote_copy(
            src_ref=src, dst_ref=dst, send_sem=send_sem, recv_sem=recv_sem,
            device_id=target, device_id_type=MESH,
        )

    def halo_copies(s):
        copies = [
            remote(stage.at[s, :, ny - 1], yrecv.at[s, 0], ysend_sem.at[s, 0], yrecv_sem.at[s, 0], y_up),
            remote(stage.at[s, :, 0], yrecv.at[s, 1], ysend_sem.at[s, 1], yrecv_sem.at[s, 1], y_down),
            remote(zsend.at[s, 0], zrecv.at[s, 0], zsend_sem.at[s, 0], zrecv_sem.at[s, 0], z_up),
            remote(zsend.at[s, 1], zrecv.at[s, 1], zsend_sem.at[s, 1], zrecv_sem.at[s, 1], z_down),
            remote(xsend.at[s], xrecv.at[s, 0], xsend_sem.at[s, 0], xrecv_sem.at[s, 0], x_up),
        ]
        if x_ways == 2:
            copies.append(
                remote(xsend.at[s], xrecv.at[s, 1], xsend_sem.at[s, 1], xrecv_sem.at[s, 1], x_down)
            )
        return copies

    lane = lax.broadcasted_iota(jnp.int32, (lines, nz, nx), 2)
    line = lax.broadcasted_iota(jnp.int32, (lines, nz, nx), 0)
    row = lax.broadcasted_iota(jnp.int32, (lines, nz, nx), 1)
    low_lane = lane == line
    high_lane = lane == line + nx // 2

    def send(s, f):
        stage[s] = f
        zsend[s, 0] = f[:, :, nz - 1, :]
        zsend[s, 1] = f[:, :, 0, :]
        flat = f.reshape(lines, nz, nx)
        packed = jnp.where(low_lane, flat[:, :, 0:1], 0.0)
        packed = packed + jnp.where(high_lane, flat[:, :, nx - 1 : nx], 0.0)
        xsend[s] = jnp.sum(packed, axis=0)
        copies = halo_copies(s)
        for copy in copies:
            copy.start()
        return copies

    def stepped(s, f, copies):
        for copy in copies:
            copy.wait_recv()
        flat = f.reshape(lines, nz, nx)
        bottom = jnp.where(gy == 0, 0.0, yrecv[s, 0])
        upper = jnp.where(gy == n_gy - 1, 0.0, yrecv[s, 1])
        y_minus = jnp.concatenate([bottom[:, None], f[:, :-1]], axis=1)
        y_plus = jnp.concatenate([f[:, 1:], upper[:, None]], axis=1)
        z_low = zrecv[s, 0].reshape(lines, 1, nx)
        z_high = zrecv[s, 1].reshape(lines, 1, nx)
        z_minus = jnp.where(row == 0, z_low, pltpu.roll(flat, 1, 1)).reshape(f.shape)
        z_plus = jnp.where(row == nz - 1, z_high, pltpu.roll(flat, nz - 1, 1)).reshape(f.shape)
        from_left, from_right = xrecv[s, 0], xrecv[s, x_ways - 1]
        x_low = jnp.sum(jnp.where(high_lane, from_left[None], 0.0), axis=2, keepdims=True)
        x_high = jnp.sum(jnp.where(low_lane, from_right[None], 0.0), axis=2, keepdims=True)
        x_minus = jnp.where(lane == 0, x_low, pltpu.roll(flat, 1, 2)).reshape(f.shape)
        x_plus = jnp.where(lane == nx - 1, x_high, pltpu.roll(flat, nx - 1, 2)).reshape(f.shape)
        carried = f[0][None] * (x_plus - x_minus) * 0.5
        carried = carried + f[1][None] * (y_plus - y_minus) * 0.5
        carried = carried + f[2][None] * (z_plus - z_minus) * 0.5
        spread = x_plus + x_minus + y_plus + y_minus + z_plus + z_minus - 6.0 * f
        return f + time_step * (viscosity * spread - carried)

    def scatter_copy(i):
        peer, target = plane_id(i + 1)
        return remote(
            gram_ref.at[peer], plane_ref.at[me], asend_sem.at[i], arecv_sem.at[me], target
        )

    def line_copy(i):
        _, target = line_id(i + 1)
        return remote(part_ref, line_ref.at[gz], bsend_sem.at[i], brecv_sem.at[gz], target)

    def gather_copy(i):
        _, target = plane_id(i + 1)
        return remote(
            full_ref.at[me], full_ref.at[me], csend_sem.at[i], crecv_sem.at[me], target
        )

    def cross_plane_copy(i):
        _, target = plane_id(i + 1)
        return remote(cross_send, cross_plane.at[me], dsend_sem.at[i], drecv_sem.at[me], target)

    def cross_line_copy(i):
        _, target = line_id(i + 1)
        return remote(cross_mid, cross_line.at[gz], esend_sem.at[i], erecv_sem.at[gz], target)

    def wait_plane(buffer, sem):
        def body(i):
            peer, target = plane_id(i + 1)
            remote(buffer.at[peer], buffer.at[peer], sem.at[peer], sem.at[peer], target).wait_recv()

        each(n_plane - 1, body)

    def wait_line(buffer, sem):
        def body(i):
            peer, target = line_id(i + 1)
            remote(buffer.at[peer], buffer.at[peer], sem.at[peer], sem.at[peer], target).wait_recv()

        each(n_gz - 1, body)

    modes, count = old_ref.shape[0], old_ref.shape[1]

    def flatten():
        for load in loads:
            load.wait()

        def scale_row(r, carry):
            wide_ref[pl.ds(r * count, count), :] = strength_ref[r] * old_ref[r].astype(jnp.float32)
            return carry

        def copy_row(r, carry):
            wide_ref[pl.ds((r + modes) * count, count), :] = snap_ref[r].astype(jnp.float32)
            return carry

        lax.fori_loop(0, modes, scale_row, 0, unroll=8)
        lax.fori_loop(0, snap_ref.shape[0], copy_row, 0, unroll=7)
        wide_ref[pl.ds((ranks - 1) * count, count), :] = jnp.zeros((count, nx), jnp.float32)
        for b in range(count):
            column = wide_ref[pl.ds(b, ranks, stride=count), :]
            earlier_ref[:, b * nx : (b + 1) * nx] = column.astype(jnp.bfloat16)

    def begin_gram():
        flatten()
        earlier = earlier_ref[...]
        gram = lax.dot_general(
            earlier, earlier, (((1,), (1,)), ((), ())), preferred_element_type=jnp.float32
        )
        gram_ref[...] = gram.reshape(gram_ref.shape)
        plane_ref[me] = gram_ref[me]
        each(n_plane - 1, lambda i: scatter_copy(i).start())

    def add_plane():
        wait_plane(plane_ref, arecv_sem)
        part = jnp.sum(plane_ref[...], axis=0)
        part_ref[...] = part
        line_ref[gz] = part
        each(n_gz - 1, lambda i: line_copy(i).start())

    def add_line():
        wait_line(line_ref, brecv_sem)
        full_ref[me] = jnp.sum(line_ref[...], axis=0)
        each(n_plane - 1, lambda i: gather_copy(i).start())

    between = {0: begin_gram, 2: add_plane, 3: add_line}
    base = v_ref[...]
    f = base
    for s in range(STAGES):
        copies = send(s, f)
        if s in between:
            between[s]()
        moved = stepped(s, f, copies)
        if s % 3 == 0:
            f = moved
        elif s % 3 == 1:
            f = 0.75 * base + 0.25 * moved
        else:
            f = base / 3.0 + 2.0 / 3.0 * moved
            base = f
    field_ref[...] = f

    blocks = [(c, y, z) for c in range(comps) for y in range(0, ny, 2) for z in range(0, nz, 2)]

    def newest_block(b):
        c, y, z = blocks[b]
        return field_ref[c, y, pl.ds(z, 1), :].astype(jnp.bfloat16).astype(jnp.float32)

    total = jnp.zeros((ranks, nx), jnp.float32)
    own = jnp.zeros((1, nx), jnp.float32)
    for b in range(len(blocks)):
        newest = newest_block(b)
        total = total + earlier_ref[:, b * nx : (b + 1) * nx].astype(jnp.float32) * newest
        own = own + newest * newest
    square_row = lax.broadcasted_iota(jnp.int32, (ranks, ranks), 0)
    square_col = lax.broadcasted_iota(jnp.int32, (ranks, ranks), 1)
    total = jnp.where(lax.broadcasted_iota(jnp.int32, (ranks, nx), 0) == ranks - 1, own, total)
    cross = jnp.sum(total.T, axis=0, keepdims=True)
    cross_send[...] = jnp.broadcast_to(cross, cross_send.shape)
    cross_plane[me] = cross_send[...]
    each(n_plane - 1, lambda i: cross_plane_copy(i).start())
    tail = slice(ranks - 16, ranks)
    last = lax.broadcasted_iota(jnp.int32, (16, nx), 0) == 15
    for b in range(len(blocks)):
        columns = slice(b * nx, (b + 1) * nx)
        rows = earlier_ref[tail, columns].astype(jnp.float32)
        earlier_ref[tail, columns] = jnp.where(last, newest_block(b), rows).astype(jnp.bfloat16)
    wait_plane(full_ref, crecv_sem)
    wait_plane(cross_plane, drecv_sem)
    cross_mid[...] = jnp.sum(cross_plane[...], axis=0)
    cross_line[gz] = cross_mid[...]
    each(n_gz - 1, lambda i: cross_line_copy(i).start())
    wait_line(cross_line, erecv_sem)
    cross = jnp.sum(cross_line[...], axis=0)[0:1]
    cross = jnp.broadcast_to(cross, (ranks, ranks))

    gram = full_ref[...].reshape(ranks, ranks)
    gram = jnp.where(square_col == ranks - 1, cross.T, gram)
    gram = jnp.where(square_row == ranks - 1, cross, gram)
    scale = jnp.sqrt(jnp.sum(gram * gram, keepdims=True))
    level = gram / scale
    ident = jnp.where(square_row == square_col, 1.0, 0.0)
    dot = functools.partial(
        jnp.dot, precision=lax.Precision.HIGHEST, preferred_element_type=jnp.float32
    )
    inverse = ident
    for repeat in range(NS_ITERS):
        product = level if repeat == 0 else dot(inverse, level)
        factor = 1.5 * ident - 0.5 * product
        level = dot(level, factor)
        inverse = factor if repeat == 0 else dot(factor, inverse)
    level_ref[...] = level
    factor = jnp.sqrt(jnp.full((1, 1), rows_total, jnp.float32)) / jnp.sqrt(scale)
    weights = (inverse * factor).astype(jnp.bfloat16)
    weights_ref[...] = weights

    for s in range(STAGES):
        for copy in halo_copies(s):
            copy.wait_send()
    each(n_plane - 1, lambda i: scatter_copy(i).wait_send())
    each(n_gz - 1, lambda i: line_copy(i).wait_send())
    each(n_plane - 1, lambda i: gather_copy(i).wait_send())
    each(n_plane - 1, lambda i: cross_plane_copy(i).wait_send())
    each(n_gz - 1, lambda i: cross_line_copy(i).wait_send())


def rotate(field_in, level_in, weights_ref, whole_ref, field_ref, level_ref, basis_ref, wide_ref):
    field_ref[...] = field_in[...]
    level_ref[...] = level_in[...]
    ranks, count, nx = basis_ref.shape
    weights = weights_ref[...]
    for b in range(count):
        wide_ref[pl.ds(b, ranks, stride=count), :] = jnp.dot(
            weights, whole_ref[:, b * nx : (b + 1) * nx], preferred_element_type=jnp.float32
        )

    def write(r, carry):
        basis_ref[r] = wide_ref[pl.ds(r * count, count), :].astype(jnp.bfloat16)
        return carry

    lax.fori_loop(0, ranks, write, 0, unroll=8)


def local(velocity, basis_old, strength, snapshots):
    modes = basis_old.shape[0]
    earlier_count = snapshots.shape[0]
    ranks = modes + earlier_count + 1
    sizes = tuple(lax.axis_size(axis) for axis in ("grp", "gy", "gz"))
    n_grp, n_gy, n_gz = sizes
    n_plane = n_grp * n_gy
    comps, ny, nz, nx = velocity.shape
    count = comps * (ny // 2) * (nz // 2)
    length = count * nx
    share = ranks // n_plane
    assert share * n_plane == ranks
    f32 = jnp.float32
    dma = pltpu.SemaphoreType.DMA
    vmem = pl.BlockSpec(memory_space=pltpu.VMEM)
    field, level, weights, whole = pl.pallas_call(
        functools.partial(kernel, sizes, float(length * n_plane * n_gz)),
        out_shape=(
            jax.ShapeDtypeStruct(velocity.shape, f32),
            jax.ShapeDtypeStruct((ranks, ranks), f32),
            jax.ShapeDtypeStruct((ranks, ranks), jnp.bfloat16),
            jax.ShapeDtypeStruct((ranks, length), jnp.bfloat16),
        ),
        in_specs=[
            vmem,
            pl.BlockSpec(memory_space=pltpu.SMEM),
            pl.BlockSpec(memory_space=pltpu.HBM),
            pl.BlockSpec(memory_space=pltpu.HBM),
        ],
        out_specs=(vmem, vmem, vmem, vmem),
        scratch_shapes=[
            pltpu.VMEM((modes, count, nx), jnp.bfloat16),
            pltpu.VMEM((earlier_count, count, nx), jnp.bfloat16),
            pltpu.VMEM((ranks * count, nx), f32),
            dma((2,)),
            pltpu.VMEM((STAGES,) + velocity.shape, f32),
            pltpu.VMEM((STAGES, 2, comps, ny, nx), f32),
            pltpu.VMEM((STAGES, nz, nx), f32),
            pltpu.VMEM((STAGES, 2, comps, nz, nx), f32),
            pltpu.VMEM((STAGES, 2, comps, ny, nx), f32),
            pltpu.VMEM((STAGES, 2, nz, nx), f32),
            pltpu.VMEM((n_plane, share, ranks), f32),
            pltpu.VMEM((share, ranks), f32),
            pltpu.VMEM((n_plane, share, ranks), f32),
            pltpu.VMEM((n_gz, share, ranks), f32),
            pltpu.VMEM((n_plane, share, ranks), f32),
            pltpu.VMEM((8, ranks), f32),
            pltpu.VMEM((n_plane, 8, ranks), f32),
            pltpu.VMEM((8, ranks), f32),
            pltpu.VMEM((n_gz, 8, ranks), f32),
            dma((STAGES, 2)), dma((STAGES, 2)),
            dma((STAGES, 2)), dma((STAGES, 2)),
            dma((STAGES, 2)), dma((STAGES, 2)),
            dma((n_plane,)), dma((n_plane,)),
            dma((n_gz,)), dma((n_gz,)),
            dma((n_plane,)), dma((n_plane,)),
            dma((n_plane,)), dma((n_plane,)),
            dma((n_gz,)), dma((n_gz,)),
        ],
        compiler_params=pltpu.CompilerParams(
            collective_id=0, has_side_effects=True, vmem_limit_bytes=24 * 1024 * 1024
        ),
    )(velocity, strength, basis_old.reshape(modes, count, nx), snapshots.reshape(earlier_count, count, nx))
    field, level, basis_new = pl.pallas_call(
        rotate,
        out_shape=(
            jax.ShapeDtypeStruct(velocity.shape, f32),
            jax.ShapeDtypeStruct((ranks, ranks), f32),
            jax.ShapeDtypeStruct((ranks, count, nx), jnp.bfloat16),
        ),
        in_specs=[vmem, vmem, vmem, vmem],
        out_specs=(vmem, vmem, vmem),
        scratch_shapes=[pltpu.VMEM((ranks * count, nx), f32)],
        compiler_params=pltpu.CompilerParams(vmem_limit_bytes=16 * 1024 * 1024),
    )(field, level, weights, whole)
    basis_new = basis_new.reshape(ranks, comps, ny // 2, nz // 2, nx)
    return (field, basis_new, level)


def solution(mesh):
    placed = (
        P(None, "gy", "gz", "grp"),
        P(None, None, "gy", "gz", "grp"),
        P(),
        P(None, None, "gy", "gz", "grp"),
    )
    return jax.shard_map(
        local,
        mesh=mesh,
        in_specs=placed,
        out_specs=(P(None, "gy", "gz", "grp"), P(None, None, "gy", "gz", "grp"), P()),
        check_vma=False,
    )
```

```python
import functools

import jax
import jax.numpy as jnp
from jax import lax
from jax.experimental import pallas as pl
from jax.experimental.pallas import tpu as pltpu
from jax.sharding import PartitionSpec as P

NS_ITERS = 8
STAGES = 6
MESH = pl.DeviceIdType.MESH

time_step = 0.1
viscosity = 0.05


def each(count, body):
    if count <= 8:
        for i in range(count):
            body(i)
    else:
        lax.fori_loop(0, count, lambda i, carry: (body(i), carry)[1], 0)


def kernel(
    sizes, rows_total, v_hbm, strength_hbm, old_hbm, snap_hbm,
    field_hbm, level_ref, weights_ref, whole_hbm,
    field_ref, earlier_ref, store_sem,
    v_ref, strength_ref, old_ref, snap_ref, wide_ref, load_sem,
    stage, zsend, xsend, yrecv, zrecv, xrecv,
    gram_ref, part_ref, plane_ref, line_ref, full_ref,
    cross_send, cross_plane, cross_mid, cross_line,
    ysend_sem, yrecv_sem, zsend_sem, zrecv_sem, xsend_sem, xrecv_sem,
    asend_sem, arecv_sem, bsend_sem, brecv_sem, csend_sem, crecv_sem,
    dsend_sem, drecv_sem, esend_sem, erecv_sem,
):
    n_grp, n_gy, n_gz = sizes
    grp, gy, gz = lax.axis_index("grp"), lax.axis_index("gy"), lax.axis_index("gz")
    n_plane = n_grp * n_gy
    me = grp * n_gy + gy
    comps, ny, nz, nx = v_ref.shape
    ranks = earlier_ref.shape[0]
    lines = comps * ny

    def plane_id(offset):
        peer = lax.rem(me + offset, n_plane)
        return peer, {"grp": peer // n_gy, "gy": lax.rem(peer, n_gy)}

    def line_id(offset):
        peer = lax.rem(gz + offset, n_gz)
        return peer, {"gz": peer}

    y_up, y_down = {"gy": lax.rem(gy + 1, n_gy)}, {"gy": lax.rem(gy + n_gy - 1, n_gy)}
    z_up, z_down = {"gz": lax.rem(gz + 1, n_gz)}, {"gz": lax.rem(gz + n_gz - 1, n_gz)}
    x_up, x_down = {"grp": lax.rem(grp + 1, n_grp)}, {"grp": lax.rem(grp + n_grp - 1, n_grp)}
    x_ways = 1 if n_grp == 2 else 2

    loads = [
        pltpu.make_async_copy(v_hbm, v_ref, load_sem.at[2]),
        pltpu.make_async_copy(strength_hbm, strength_ref, load_sem.at[3]),
        pltpu.make_async_copy(old_hbm, old_ref, load_sem.at[0]),
        pltpu.make_async_copy(snap_hbm, snap_ref, load_sem.at[1]),
    ]
    for load in loads:
        load.start()
    barrier = pltpu.get_barrier_semaphore()

    def greet_plane(i):
        pl.semaphore_signal(barrier, inc=1, device_id=plane_id(i + 1)[1], device_id_type=MESH)

    def greet_line(i):
        pl.semaphore_signal(barrier, inc=1, device_id=line_id(i + 1)[1], device_id_type=MESH)

    each(n_plane - 1, greet_plane)
    each(n_gz - 1, greet_line)
    pl.semaphore_wait(barrier, n_plane + n_gz - 2)

    def remote(src, dst, send_sem, recv_sem, target):
        return pltpu.make_async_remote_copy(
            src_ref=src, dst_ref=dst, send_sem=send_sem, recv_sem=recv_sem,
            device_id=target, device_id_type=MESH,
        )

    def halo_copies(s):
        copies = [
            remote(stage.at[s, :, ny - 1], yrecv.at[s, 0], ysend_sem.at[s, 0], yrecv_sem.at[s, 0], y_up),
            remote(stage.at[s, :, 0], yrecv.at[s, 1], ysend_sem.at[s, 1], yrecv_sem.at[s, 1], y_down),
            remote(zsend.at[s, 0], zrecv.at[s, 0], zsend_sem.at[s, 0], zrecv_sem.at[s, 0], z_up),
            remote(zsend.at[s, 1], zrecv.at[s, 1], zsend_sem.at[s, 1], zrecv_sem.at[s, 1], z_down),
            remote(xsend.at[s], xrecv.at[s, 0], xsend_sem.at[s, 0], xrecv_sem.at[s, 0], x_up),
        ]
        if x_ways == 2:
            copies.append(
                remote(xsend.at[s], xrecv.at[s, 1], xsend_sem.at[s, 1], xrecv_sem.at[s, 1], x_down)
            )
        return copies

    lane = lax.broadcasted_iota(jnp.int32, (lines, nz, nx), 2)
    line = lax.broadcasted_iota(jnp.int32, (lines, nz, nx), 0)
    row = lax.broadcasted_iota(jnp.int32, (lines, nz, nx), 1)
    low_lane = lane == line
    high_lane = lane == line + nx // 2

    def send(s, f):
        copies = halo_copies(s)
        zsend[s, 0] = f[:, :, nz - 1, :]
        zsend[s, 1] = f[:, :, 0, :]
        for copy in copies[2:4]:
            copy.start()
        stage[s] = f
        for copy in copies[:2]:
            copy.start()
        flat = f.reshape(lines, nz, nx)
        packed = jnp.where(low_lane, flat[:, :, 0:1], 0.0)
        packed = jnp.where(high_lane, flat[:, :, nx - 1 : nx], packed)
        xsend[s] = jnp.sum(packed, axis=0)
        for copy in copies[4:]:
            copy.start()
        return copies

    def stepped(s, f, copies):
        flat = f.reshape(lines, nz, nx)
        left, right = pltpu.roll(flat, 1, 2), pltpu.roll(flat, nx - 1, 2)
        below, above = pltpu.roll(flat, 1, 1), pltpu.roll(flat, nz - 1, 1)
        for copy in copies[:2]:
            copy.wait_recv()
        bottom = jnp.where(gy == 0, 0.0, yrecv[s, 0])
        upper = jnp.where(gy == n_gy - 1, 0.0, yrecv[s, 1])
        y_minus = jnp.concatenate([bottom[:, None], f[:, :-1]], axis=1)
        y_plus = jnp.concatenate([f[:, 1:], upper[:, None]], axis=1)
        carried = f[1][None] * (y_plus - y_minus) * 0.5
        spread = y_plus + y_minus - 6.0 * f
        for copy in copies[4:]:
            copy.wait_recv()
        from_left, from_right = xrecv[s, 0], xrecv[s, x_ways - 1]
        x_low = jnp.sum(jnp.where(high_lane, from_left[None], 0.0), axis=2, keepdims=True)
        x_high = jnp.sum(jnp.where(low_lane, from_right[None], 0.0), axis=2, keepdims=True)
        x_minus = jnp.where(lane == 0, x_low, left).reshape(f.shape)
        x_plus = jnp.where(lane == nx - 1, x_high, right).reshape(f.shape)
        carried = carried + f[0][None] * (x_plus - x_minus) * 0.5
        spread = spread + (x_plus + x_minus)
        for copy in copies[2:4]:
            copy.wait_recv()
        z_low = zrecv[s, 0].reshape(lines, 1, nx)
        z_high = zrecv[s, 1].reshape(lines, 1, nx)
        z_minus = jnp.where(row == 0, z_low, below).reshape(f.shape)
        z_plus = jnp.where(row == nz - 1, z_high, above).reshape(f.shape)
        carried = carried + f[2][None] * (z_plus - z_minus) * 0.5
        spread = spread + (z_plus + z_minus)
        return f + time_step * (viscosity * spread - carried)

    def scatter_copy(i):
        peer, target = plane_id(i + 1)
        return remote(
            gram_ref.at[peer], plane_ref.at[me], asend_sem.at[i], arecv_sem.at[me], target
        )

    def line_copy(i):
        _, target = line_id(i + 1)
        return remote(part_ref, line_ref.at[gz], bsend_sem.at[i], brecv_sem.at[gz], target)

    def gather_copy(i):
        _, target = plane_id(i + 1)
        return remote(
            full_ref.at[me], full_ref.at[me], csend_sem.at[i], crecv_sem.at[me], target
        )

    def cross_plane_copy(i):
        _, target = plane_id(i + 1)
        return remote(cross_send, cross_plane.at[me], dsend_sem.at[i], drecv_sem.at[me], target)

    def cross_line_copy(i):
        _, target = line_id(i + 1)
        return remote(cross_mid, cross_line.at[gz], esend_sem.at[i], erecv_sem.at[gz], target)

    def wait_plane(buffer, sem):
        def body(i):
            peer, target = plane_id(i + 1)
            remote(buffer.at[peer], buffer.at[peer], sem.at[peer], sem.at[peer], target).wait_recv()

        each(n_plane - 1, body)

    def wait_line(buffer, sem):
        def body(i):
            peer, target = line_id(i + 1)
            remote(buffer.at[peer], buffer.at[peer], sem.at[peer], sem.at[peer], target).wait_recv()

        each(n_gz - 1, body)

    modes, count = old_ref.shape[0], old_ref.shape[1]

    def flatten_old():
        for load in loads[1:]:
            load.wait()

        def scale_row(r, carry):
            wide_ref[pl.ds(r * count, count), :] = strength_ref[r] * old_ref[r].astype(jnp.float32)
            return carry

        lax.fori_loop(0, modes, scale_row, 0, unroll=8)

    def flatten_snapshots():
        def copy_row(r, carry):
            wide_ref[pl.ds((r + modes) * count, count), :] = snap_ref[r].astype(jnp.float32)
            return carry

        lax.fori_loop(0, snap_ref.shape[0], copy_row, 0, unroll=7)
        wide_ref[pl.ds((ranks - 1) * count, count), :] = jnp.zeros((count, nx), jnp.float32)
        take_columns(0, count // 2)

    def take_columns(first, stop):
        for b in range(first, stop):
            column = wide_ref[pl.ds(b, ranks, stride=count), :]
            earlier_ref[:, b * nx : (b + 1) * nx] = column.astype(jnp.bfloat16)

    def begin_gram():
        take_columns(count // 2, count)
        earlier = earlier_ref[...]
        gram = lax.dot_general(
            earlier, earlier, (((1,), (1,)), ((), ())), preferred_element_type=jnp.float32
        )
        gram_ref[...] = gram.reshape(gram_ref.shape)
        plane_ref[me] = gram_ref[me]
        each(n_plane - 1, lambda i: scatter_copy(i).start())

    def add_plane():
        wait_plane(plane_ref, arecv_sem)
        part = jnp.sum(plane_ref[...], axis=0)
        part_ref[...] = part
        line_ref[gz] = part
        each(n_gz - 1, lambda i: line_copy(i).start())

    def add_line():
        wait_line(line_ref, brecv_sem)
        full_ref[me] = jnp.sum(line_ref[...], axis=0)
        each(n_plane - 1, lambda i: gather_copy(i).start())

    between = {0: flatten_old, 1: flatten_snapshots, 2: begin_gram, 3: add_plane, 4: add_line}
    loads[0].wait()
    base = v_ref[...]
    f = base
    for s in range(STAGES):
        copies = send(s, f)
        if s in between:
            between[s]()
        moved = stepped(s, f, copies)
        if s % 3 == 0:
            f = moved
        elif s % 3 == 1:
            f = 0.75 * base + 0.25 * moved
        else:
            f = base / 3.0 + 2.0 / 3.0 * moved
            base = f
    field_ref[...] = f
    field_store = pltpu.make_async_copy(field_ref, field_hbm, store_sem.at[0])
    field_store.start()

    blocks = [(c, y, z) for c in range(comps) for y in range(0, ny, 2) for z in range(0, nz, 2)]

    def newest_block(b):
        c, y, z = blocks[b]
        return field_ref[c, y, pl.ds(z, 1), :].astype(jnp.bfloat16).astype(jnp.float32)

    total = jnp.zeros((ranks, nx), jnp.float32)
    own = jnp.zeros((1, nx), jnp.float32)
    for b in range(len(blocks)):
        newest = newest_block(b)
        total = total + earlier_ref[:, b * nx : (b + 1) * nx].astype(jnp.float32) * newest
        own = own + newest * newest
    square_row = lax.broadcasted_iota(jnp.int32, (ranks, ranks), 0)
    square_col = lax.broadcasted_iota(jnp.int32, (ranks, ranks), 1)
    total = jnp.where(lax.broadcasted_iota(jnp.int32, (ranks, nx), 0) == ranks - 1, own, total)
    cross = jnp.sum(total.T, axis=0, keepdims=True)
    cross_send[...] = jnp.broadcast_to(cross, cross_send.shape)
    cross_plane[me] = cross_send[...]
    each(n_plane - 1, lambda i: cross_plane_copy(i).start())
    tail = slice(ranks - 16, ranks)
    last = lax.broadcasted_iota(jnp.int32, (16, nx), 0) == 15
    for b in range(len(blocks)):
        columns = slice(b * nx, (b + 1) * nx)
        rows = earlier_ref[tail, columns].astype(jnp.float32)
        earlier_ref[tail, columns] = jnp.where(last, newest_block(b), rows).astype(jnp.bfloat16)
    whole_store = pltpu.make_async_copy(earlier_ref, whole_hbm, store_sem.at[1])
    whole_store.start()
    wait_plane(full_ref, crecv_sem)
    wait_plane(cross_plane, drecv_sem)
    cross_mid[...] = jnp.sum(cross_plane[...], axis=0)
    cross_line[gz] = cross_mid[...]
    each(n_gz - 1, lambda i: cross_line_copy(i).start())
    wait_line(cross_line, erecv_sem)
    cross = jnp.sum(cross_line[...], axis=0)[0:1]
    cross = jnp.broadcast_to(cross, (ranks, ranks))

    gram = full_ref[...].reshape(ranks, ranks)
    gram = jnp.where(square_col == ranks - 1, cross.T, gram)
    gram = jnp.where(square_row == ranks - 1, cross, gram)
    scale = jnp.sqrt(jnp.sum(gram * gram, keepdims=True))
    level = gram / scale
    ident = jnp.where(square_row == square_col, 1.0, 0.0)

    def split(a):
        coarse = a.astype(jnp.bfloat16)
        return coarse, (a - coarse.astype(jnp.float32)).astype(jnp.bfloat16)

    def dot(left, right):
        terms = jnp.concatenate(right, axis=1)
        both = jnp.dot(
            jnp.concatenate(left, axis=1),
            jnp.concatenate([terms, terms], axis=0),
            preferred_element_type=jnp.float32,
        )
        return both[:, :ranks] + both[:, ranks:]

    inverse, inverse_split = ident, None
    for repeat in range(NS_ITERS):
        level_split = split(level)
        product = level if repeat == 0 else dot(inverse_split, level_split)
        factor = 1.5 * ident - 0.5 * product
        factor_split = split(factor)
        inverse = factor if repeat == 0 else dot(factor_split, inverse_split)
        level = dot(level_split, factor_split)
        inverse_split = split(inverse)
    level_ref[...] = level
    factor = jnp.sqrt(jnp.full((1, 1), rows_total, jnp.float32)) / jnp.sqrt(scale)
    weights = (inverse * factor).astype(jnp.bfloat16)
    weights_ref[...] = weights

    field_store.wait()
    whole_store.wait()
    for s in range(STAGES):
        for copy in halo_copies(s):
            copy.wait_send()
    each(n_plane - 1, lambda i: scatter_copy(i).wait_send())
    each(n_gz - 1, lambda i: line_copy(i).wait_send())
    each(n_plane - 1, lambda i: gather_copy(i).wait_send())
    each(n_plane - 1, lambda i: cross_plane_copy(i).wait_send())
    each(n_gz - 1, lambda i: cross_line_copy(i).wait_send())


def rotate(
    field_in, level_in, weights_in, whole_in, field_out, level_out, basis_out,
    weights_ref, whole_ref, wide_ref, basis_ref, pass_sem, load_sem, store_sem,
):
    ranks, count, nx = basis_ref.shape
    parts = load_sem.shape[0] - 1
    width = count // parts * nx
    loads = [pltpu.make_async_copy(weights_in, weights_ref, load_sem.at[parts])]
    for p in range(parts):
        columns = (slice(None), pl.ds(p * width, width))
        loads.append(pltpu.make_async_copy(whole_in.at[columns], whole_ref.at[columns], load_sem.at[p]))
    passes = [
        pltpu.make_async_copy(field_in, field_out, pass_sem.at[0]),
        pltpu.make_async_copy(level_in, level_out, pass_sem.at[1]),
    ]
    for copy in loads + passes:
        copy.start()
    loads[0].wait()
    weights = weights_ref[...]
    for p in range(parts):
        loads[p + 1].wait()
        for b in range(p * count // parts, (p + 1) * count // parts, 2):
            pair = jnp.dot(
                weights, whole_ref[:, b * nx : (b + 2) * nx], preferred_element_type=jnp.float32
            )
            wide_ref[pl.ds(b, ranks, stride=count), :] = pair[:, :nx]
            wide_ref[pl.ds(b + 1, ranks, stride=count), :] = pair[:, nx:]
    pieces = store_sem.shape[0]
    depth = ranks // pieces
    stores = []
    for p in range(pieces):
        rows = pl.ds(p * depth, depth)
        piece = wide_ref[pl.ds(p * depth * count, depth * count), :].astype(jnp.bfloat16)
        basis_ref[rows] = piece.reshape(depth, count, nx)
        stores.append(pltpu.make_async_copy(basis_ref.at[rows], basis_out.at[rows], store_sem.at[p]))
        stores[-1].start()
    for copy in passes + stores:
        copy.wait()


def local(velocity, basis_old, strength, snapshots):
    modes = basis_old.shape[0]
    earlier_count = snapshots.shape[0]
    ranks = modes + earlier_count + 1
    sizes = tuple(lax.axis_size(axis) for axis in ("grp", "gy", "gz"))
    n_grp, n_gy, n_gz = sizes
    n_plane = n_grp * n_gy
    comps, ny, nz, nx = velocity.shape
    count = comps * (ny // 2) * (nz // 2)
    length = count * nx
    share = ranks // n_plane
    assert share * n_plane == ranks
    f32 = jnp.float32
    dma = pltpu.SemaphoreType.DMA
    vmem = pl.BlockSpec(memory_space=pltpu.VMEM)
    hbm = pl.BlockSpec(memory_space=pltpu.HBM)
    field, level, weights, whole = pl.pallas_call(
        functools.partial(kernel, sizes, float(length * n_plane * n_gz)),
        out_shape=(
            jax.ShapeDtypeStruct(velocity.shape, f32),
            jax.ShapeDtypeStruct((ranks, ranks), f32),
            jax.ShapeDtypeStruct((ranks, ranks), jnp.bfloat16),
            jax.ShapeDtypeStruct((ranks, length), jnp.bfloat16),
        ),
        in_specs=[
            hbm,
            hbm,
            hbm,
            hbm,
        ],
        out_specs=(hbm, vmem, vmem, hbm),
        scratch_shapes=[
            pltpu.VMEM(velocity.shape, f32),
            pltpu.VMEM((ranks, length), jnp.bfloat16),
            dma((2,)),
            pltpu.VMEM(velocity.shape, f32),
            pltpu.SMEM((modes,), f32),
            pltpu.VMEM((modes, count, nx), jnp.bfloat16),
            pltpu.VMEM((earlier_count, count, nx), jnp.bfloat16),
            pltpu.VMEM((ranks * count, nx), f32),
            dma((4,)),
            pltpu.VMEM((STAGES,) + velocity.shape, f32),
            pltpu.VMEM((STAGES, 2, comps, ny, nx), f32),
            pltpu.VMEM((STAGES, nz, nx), f32),
            pltpu.VMEM((STAGES, 2, comps, nz, nx), f32),
            pltpu.VMEM((STAGES, 2, comps, ny, nx), f32),
            pltpu.VMEM((STAGES, 2, nz, nx), f32),
            pltpu.VMEM((n_plane, share, ranks), f32),
            pltpu.VMEM((share, ranks), f32),
            pltpu.VMEM((n_plane, share, ranks), f32),
            pltpu.VMEM((n_gz, share, ranks), f32),
            pltpu.VMEM((n_plane, share, ranks), f32),
            pltpu.VMEM((8, ranks), f32),
            pltpu.VMEM((n_plane, 8, ranks), f32),
            pltpu.VMEM((8, ranks), f32),
            pltpu.VMEM((n_gz, 8, ranks), f32),
            dma((STAGES, 2)), dma((STAGES, 2)),
            dma((STAGES, 2)), dma((STAGES, 2)),
            dma((STAGES, 2)), dma((STAGES, 2)),
            dma((n_plane,)), dma((n_plane,)),
            dma((n_gz,)), dma((n_gz,)),
            dma((n_plane,)), dma((n_plane,)),
            dma((n_plane,)), dma((n_plane,)),
            dma((n_gz,)), dma((n_gz,)),
        ],
        compiler_params=pltpu.CompilerParams(
            collective_id=0, has_side_effects=True, vmem_limit_bytes=56 * 1024 * 1024
        ),
    )(velocity, strength, basis_old.reshape(modes, count, nx), snapshots.reshape(earlier_count, count, nx))
    field, level, basis_new = pl.pallas_call(
        rotate,
        out_shape=(
            jax.ShapeDtypeStruct(velocity.shape, f32),
            jax.ShapeDtypeStruct((ranks, ranks), f32),
            jax.ShapeDtypeStruct((ranks, count, nx), jnp.bfloat16),
        ),
        in_specs=[hbm] * 4,
        out_specs=(hbm,) * 3,
        scratch_shapes=[
            pltpu.VMEM((ranks, ranks), jnp.bfloat16),
            pltpu.VMEM((ranks, length), jnp.bfloat16),
            pltpu.VMEM((ranks * count, nx), f32),
            pltpu.VMEM((ranks, count, nx), jnp.bfloat16),
            dma((2,)),
            dma((5,)),
            dma((4,)),
        ],
        compiler_params=pltpu.CompilerParams(vmem_limit_bytes=56 * 1024 * 1024),
    )(field, level, weights, whole)
    basis_new = basis_new.reshape(ranks, comps, ny // 2, nz // 2, nx)
    return (field, basis_new, level)


def solution(mesh):
    placed = (
        P(None, "gy", "gz", "grp"),
        P(None, None, "gy", "gz", "grp"),
        P(),
        P(None, None, "gy", "gz", "grp"),
    )
    return jax.shard_map(
        local,
        mesh=mesh,
        in_specs=placed,
        out_specs=(P(None, "gy", "gz", "grp"), P(None, None, "gy", "gz", "grp"), P()),
        check_vma=False,
    )
```

```python
import functools

import jax
import jax.numpy as jnp
from jax import lax
from jax.experimental import pallas as pl
from jax.experimental.pallas import tpu as pltpu
from jax.sharding import PartitionSpec as P

NS_ITERS = 8
STAGES = 6
MESH = pl.DeviceIdType.MESH

time_step = 0.1
viscosity = 0.05


def each(count, body):
    if count <= 8:
        for i in range(count):
            body(i)
    else:
        lax.fori_loop(0, count, lambda i, carry: (body(i), carry)[1], 0)


def kernel(
    sizes, rows_total, v_hbm, strength_hbm, old_hbm, snap_hbm,
    field_hbm, level_ref, weights_ref, whole_hbm,
    field_ref, earlier_ref, store_sem,
    v_ref, strength_ref, old_ref, snap_ref, wide_ref, load_sem,
    stage, zsend, xsend, yrecv, zrecv, xrecv,
    gram_ref, part_ref, plane_ref, line_ref, full_ref,
    cross_send, cross_plane, cross_mid, cross_line,
    ysend_sem, yrecv_sem, zsend_sem, zrecv_sem, xsend_sem, xrecv_sem,
    asend_sem, arecv_sem, bsend_sem, brecv_sem, csend_sem, crecv_sem,
    dsend_sem, drecv_sem, esend_sem, erecv_sem,
):
    n_grp, n_gy, n_gz = sizes
    grp, gy, gz = lax.axis_index("grp"), lax.axis_index("gy"), lax.axis_index("gz")
    n_plane = n_grp * n_gy
    me = grp * n_gy + gy
    comps, ny, nz, nx = v_ref.shape
    ranks = earlier_ref.shape[0]
    lines = comps * ny

    def plane_id(offset):
        peer = lax.rem(me + offset, n_plane)
        return peer, {"grp": peer // n_gy, "gy": lax.rem(peer, n_gy)}

    def line_id(offset):
        peer = lax.rem(gz + offset, n_gz)
        return peer, {"gz": peer}

    y_up, y_down = {"gy": lax.rem(gy + 1, n_gy)}, {"gy": lax.rem(gy + n_gy - 1, n_gy)}
    z_up, z_down = {"gz": lax.rem(gz + 1, n_gz)}, {"gz": lax.rem(gz + n_gz - 1, n_gz)}
    x_up, x_down = {"grp": lax.rem(grp + 1, n_grp)}, {"grp": lax.rem(grp + n_grp - 1, n_grp)}
    x_ways = 1 if n_grp == 2 else 2

    loads = [
        pltpu.make_async_copy(v_hbm, v_ref, load_sem.at[2]),
        pltpu.make_async_copy(strength_hbm, strength_ref, load_sem.at[3]),
        pltpu.make_async_copy(old_hbm, old_ref, load_sem.at[0]),
        pltpu.make_async_copy(snap_hbm, snap_ref, load_sem.at[1]),
    ]
    for load in loads:
        load.start()
    barrier = pltpu.get_barrier_semaphore()

    def greet_plane(i):
        pl.semaphore_signal(barrier, inc=1, device_id=plane_id(i + 1)[1], device_id_type=MESH)

    def greet_line(i):
        pl.semaphore_signal(barrier, inc=1, device_id=line_id(i + 1)[1], device_id_type=MESH)

    each(n_plane - 1, greet_plane)
    each(n_gz - 1, greet_line)
    pl.semaphore_wait(barrier, n_plane + n_gz - 2)

    def remote(src, dst, send_sem, recv_sem, target):
        return pltpu.make_async_remote_copy(
            src_ref=src, dst_ref=dst, send_sem=send_sem, recv_sem=recv_sem,
            device_id=target, device_id_type=MESH,
        )

    def halo_copies(s):
        copies = [
            remote(stage.at[s, :, ny - 1], yrecv.at[s, 0], ysend_sem.at[s, 0], yrecv_sem.at[s, 0], y_up),
            remote(stage.at[s, :, 0], yrecv.at[s, 1], ysend_sem.at[s, 1], yrecv_sem.at[s, 1], y_down),
            remote(zsend.at[s, 0], zrecv.at[s, 0], zsend_sem.at[s, 0], zrecv_sem.at[s, 0], z_up),
            remote(zsend.at[s, 1], zrecv.at[s, 1], zsend_sem.at[s, 1], zrecv_sem.at[s, 1], z_down),
            remote(xsend.at[s], xrecv.at[s, 0], xsend_sem.at[s, 0], xrecv_sem.at[s, 0], x_up),
        ]
        if x_ways == 2:
            copies.append(
                remote(xsend.at[s], xrecv.at[s, 1], xsend_sem.at[s, 1], xrecv_sem.at[s, 1], x_down)
            )
        return copies

    lane = lax.broadcasted_iota(jnp.int32, (lines, nz, nx), 2)
    line = lax.broadcasted_iota(jnp.int32, (lines, nz, nx), 0)
    row = lax.broadcasted_iota(jnp.int32, (lines, nz, nx), 1)
    low_lane = lane == line
    high_lane = lane == line + nx // 2

    def send(s, f):
        copies = halo_copies(s)
        zsend[s, 0] = f[:, :, nz - 1, :]
        zsend[s, 1] = f[:, :, 0, :]
        for copy in copies[2:4]:
            copy.start()
        stage[s] = f
        for copy in copies[:2]:
            copy.start()
        flat = f.reshape(lines, nz, nx)
        packed = jnp.where(low_lane, flat[:, :, 0:1], 0.0)
        packed = jnp.where(high_lane, flat[:, :, nx - 1 : nx], packed)
        xsend[s] = jnp.sum(packed, axis=0)
        for copy in copies[4:]:
            copy.start()
        return copies

    def stepped(s, f, copies):
        flat = f.reshape(lines, nz, nx)
        left, right = pltpu.roll(flat, 1, 2), pltpu.roll(flat, nx - 1, 2)
        below, above = pltpu.roll(flat, 1, 1), pltpu.roll(flat, nz - 1, 1)
        for copy in copies[:2]:
            copy.wait_recv()
        bottom = jnp.where(gy == 0, 0.0, yrecv[s, 0])
        upper = jnp.where(gy == n_gy - 1, 0.0, yrecv[s, 1])
        y_minus = jnp.concatenate([bottom[:, None], f[:, :-1]], axis=1)
        y_plus = jnp.concatenate([f[:, 1:], upper[:, None]], axis=1)
        carried = f[1][None] * (y_plus - y_minus) * 0.5
        spread = y_plus + y_minus - 6.0 * f
        for copy in copies[4:]:
            copy.wait_recv()
        from_left, from_right = xrecv[s, 0], xrecv[s, x_ways - 1]
        x_low = jnp.sum(jnp.where(high_lane, from_left[None], 0.0), axis=2, keepdims=True)
        x_high = jnp.sum(jnp.where(low_lane, from_right[None], 0.0), axis=2, keepdims=True)
        x_minus = jnp.where(lane == 0, x_low, left).reshape(f.shape)
        x_plus = jnp.where(lane == nx - 1, x_high, right).reshape(f.shape)
        carried = carried + f[0][None] * (x_plus - x_minus) * 0.5
        spread = spread + (x_plus + x_minus)
        for copy in copies[2:4]:
            copy.wait_recv()
        z_low = zrecv[s, 0].reshape(lines, 1, nx)
        z_high = zrecv[s, 1].reshape(lines, 1, nx)
        z_minus = jnp.where(row == 0, z_low, below).reshape(f.shape)
        z_plus = jnp.where(row == nz - 1, z_high, above).reshape(f.shape)
        carried = carried + f[2][None] * (z_plus - z_minus) * 0.5
        spread = spread + (z_plus + z_minus)
        return f + time_step * (viscosity * spread - carried)

    def scatter_copy(i):
        peer, target = plane_id(i + 1)
        return remote(
            gram_ref.at[peer], plane_ref.at[me], asend_sem.at[i], arecv_sem.at[me], target
        )

    def line_copy(i):
        _, target = line_id(i + 1)
        return remote(part_ref, line_ref.at[gz], bsend_sem.at[i], brecv_sem.at[gz], target)

    def gather_copy(i):
        _, target = plane_id(i + 1)
        return remote(
            full_ref.at[me], full_ref.at[me], csend_sem.at[i], crecv_sem.at[me], target
        )

    def cross_plane_copy(i):
        _, target = plane_id(i + 1)
        return remote(cross_send, cross_plane.at[me], dsend_sem.at[i], drecv_sem.at[me], target)

    def cross_line_copy(i):
        _, target = line_id(i + 1)
        return remote(cross_mid, cross_line.at[gz], esend_sem.at[i], erecv_sem.at[gz], target)

    def wait_plane(buffer, sem):
        def body(i):
            peer, target = plane_id(i + 1)
            remote(buffer.at[peer], buffer.at[peer], sem.at[peer], sem.at[peer], target).wait_recv()

        each(n_plane - 1, body)

    def wait_line(buffer, sem):
        def body(i):
            peer, target = line_id(i + 1)
            remote(buffer.at[peer], buffer.at[peer], sem.at[peer], sem.at[peer], target).wait_recv()

        each(n_gz - 1, body)

    modes, count = old_ref.shape[0], old_ref.shape[1]

    def flatten_old():
        for load in loads[1:]:
            load.wait()

        def scale_row(r, carry):
            wide_ref[pl.ds(r * count, count), :] = strength_ref[r] * old_ref[r].astype(jnp.float32)
            return carry

        lax.fori_loop(0, modes, scale_row, 0, unroll=8)

    def flatten_snapshots():
        def copy_row(r, carry):
            wide_ref[pl.ds((r + modes) * count, count), :] = snap_ref[r].astype(jnp.float32)
            return carry

        lax.fori_loop(0, snap_ref.shape[0], copy_row, 0, unroll=7)
        wide_ref[pl.ds((ranks - 1) * count, count), :] = jnp.zeros((count, nx), jnp.float32)
        take_columns(0, count // 2)

    def take_columns(first, stop):
        for b in range(first, stop):
            column = wide_ref[pl.ds(b, ranks, stride=count), :]
            earlier_ref[:, b * nx : (b + 1) * nx] = column.astype(jnp.bfloat16)

    def begin_gram():
        take_columns(count // 2, count)
        earlier = earlier_ref[...]
        gram = lax.dot_general(
            earlier, earlier, (((1,), (1,)), ((), ())), preferred_element_type=jnp.float32
        )
        gram_ref[...] = gram.reshape(gram_ref.shape)
        plane_ref[me] = gram_ref[me]
        each(n_plane - 1, lambda i: scatter_copy(i).start())

    def add_plane():
        wait_plane(plane_ref, arecv_sem)
        part = jnp.sum(plane_ref[...], axis=0)
        part_ref[...] = part
        line_ref[gz] = part
        each(n_gz - 1, lambda i: line_copy(i).start())

    def add_line():
        wait_line(line_ref, brecv_sem)
        full_ref[me] = jnp.sum(line_ref[...], axis=0)
        each(n_plane - 1, lambda i: gather_copy(i).start())

    between = {0: flatten_old, 1: flatten_snapshots, 2: begin_gram, 3: add_plane, 4: add_line}
    loads[0].wait()
    base = v_ref[...]
    f = base
    for s in range(STAGES):
        copies = send(s, f)
        if s in between:
            between[s]()
        moved = stepped(s, f, copies)
        if s % 3 == 0:
            f = moved
        elif s % 3 == 1:
            f = 0.75 * base + 0.25 * moved
        else:
            f = base / 3.0 + 2.0 / 3.0 * moved
            base = f
    field_ref[...] = f
    field_store = pltpu.make_async_copy(field_ref, field_hbm, store_sem.at[0])
    field_store.start()

    blocks = [(c, y, z) for c in range(comps) for y in range(0, ny, 2) for z in range(0, nz, 2)]

    def newest_block(b):
        c, y, z = blocks[b]
        return field_ref[c, y, pl.ds(z, 1), :].astype(jnp.bfloat16).astype(jnp.float32)

    total = jnp.zeros((ranks, nx), jnp.float32)
    own = jnp.zeros((1, nx), jnp.float32)
    for b in range(len(blocks)):
        newest = newest_block(b)
        total = total + earlier_ref[:, b * nx : (b + 1) * nx].astype(jnp.float32) * newest
        own = own + newest * newest
    square_row = lax.broadcasted_iota(jnp.int32, (ranks, ranks), 0)
    square_col = lax.broadcasted_iota(jnp.int32, (ranks, ranks), 1)
    total = jnp.where(lax.broadcasted_iota(jnp.int32, (ranks, nx), 0) == ranks - 1, own, total)
    cross = jnp.sum(total.T, axis=0, keepdims=True)
    cross_send[...] = jnp.broadcast_to(cross, cross_send.shape)
    cross_plane[me] = cross_send[...]
    each(n_plane - 1, lambda i: cross_plane_copy(i).start())
    tail = slice(ranks - 16, ranks)
    last = lax.broadcasted_iota(jnp.int32, (16, nx), 0) == 15
    for b in range(len(blocks)):
        columns = slice(b * nx, (b + 1) * nx)
        rows = earlier_ref[tail, columns].astype(jnp.float32)
        earlier_ref[tail, columns] = jnp.where(last, newest_block(b), rows).astype(jnp.bfloat16)
    whole_store = pltpu.make_async_copy(earlier_ref, whole_hbm, store_sem.at[1])
    whole_store.start()
    wait_plane(full_ref, crecv_sem)
    wait_plane(cross_plane, drecv_sem)
    cross_mid[...] = jnp.sum(cross_plane[...], axis=0)
    cross_line[gz] = cross_mid[...]
    each(n_gz - 1, lambda i: cross_line_copy(i).start())
    wait_line(cross_line, erecv_sem)
    cross = jnp.sum(cross_line[...], axis=0)[0:1]
    cross = jnp.broadcast_to(cross, (ranks, ranks))

    gram = full_ref[...].reshape(ranks, ranks)
    gram = jnp.where(square_col == ranks - 1, cross.T, gram)
    gram = jnp.where(square_row == ranks - 1, cross, gram)
    scale = jnp.sqrt(jnp.sum(gram * gram, keepdims=True))
    level = gram / scale
    ident = jnp.where(square_row == square_col, 1.0, 0.0)

    def split(a):
        coarse = a.astype(jnp.bfloat16)
        return coarse, (a - coarse.astype(jnp.float32)).astype(jnp.bfloat16)

    def dot(left, right):
        terms = jnp.concatenate(right, axis=1)
        both = jnp.dot(
            jnp.concatenate(left, axis=1),
            jnp.concatenate([terms, terms], axis=0),
            preferred_element_type=jnp.float32,
        )
        return both[:, :ranks] + both[:, ranks:]

    inverse, inverse_split = ident, None
    for repeat in range(NS_ITERS):
        level_split = split(level)
        product = level if repeat == 0 else dot(inverse_split, level_split)
        product_split = split(product)
        moved = product if repeat == 0 else dot(product_split, inverse_split)
        inverse = 1.5 * inverse - 0.5 * moved
        level = 1.5 * level - 0.5 * dot(level_split, product_split)
        inverse_split = split(inverse)
    level_ref[...] = level
    factor = jnp.sqrt(jnp.full((1, 1), rows_total, jnp.float32)) / jnp.sqrt(scale)
    weights = (inverse * factor).astype(jnp.bfloat16)
    weights_ref[...] = weights

    field_store.wait()
    whole_store.wait()
    for s in range(STAGES):
        for copy in halo_copies(s):
            copy.wait_send()
    each(n_plane - 1, lambda i: scatter_copy(i).wait_send())
    each(n_gz - 1, lambda i: line_copy(i).wait_send())
    each(n_plane - 1, lambda i: gather_copy(i).wait_send())
    each(n_plane - 1, lambda i: cross_plane_copy(i).wait_send())
    each(n_gz - 1, lambda i: cross_line_copy(i).wait_send())


def rotate(
    field_in, level_in, weights_in, whole_in, field_out, level_out, basis_out,
    field_ref, level_ref, weights_ref, whole_ref, wide_ref, basis_ref, pass_sem, load_sem, store_sem,
):
    ranks, count, nx = basis_ref.shape
    parts = load_sem.shape[0] - 1
    width = count // parts * nx
    loads = [pltpu.make_async_copy(weights_in, weights_ref, load_sem.at[parts])]
    for p in range(parts):
        columns = (slice(None), pl.ds(p * width, width))
        loads.append(pltpu.make_async_copy(whole_in.at[columns], whole_ref.at[columns], load_sem.at[p]))
    arrivals = [
        pltpu.make_async_copy(field_in, field_ref, pass_sem.at[0]),
        pltpu.make_async_copy(level_in, level_ref, pass_sem.at[1]),
    ]
    passes = [
        pltpu.make_async_copy(field_ref, field_out, pass_sem.at[2]),
        pltpu.make_async_copy(level_ref, level_out, pass_sem.at[3]),
    ]
    for copy in loads + arrivals:
        copy.start()
    loads[0].wait()
    weights = weights_ref[...]
    for p in range(parts):
        loads[p + 1].wait()
        for b in range(p * count // parts, (p + 1) * count // parts, 2):
            pair = jnp.dot(
                weights, whole_ref[:, b * nx : (b + 2) * nx], preferred_element_type=jnp.float32
            )
            wide_ref[pl.ds(b, ranks, stride=count), :] = pair[:, :nx]
            wide_ref[pl.ds(b + 1, ranks, stride=count), :] = pair[:, nx:]
    for arrival, copy in zip(arrivals, passes):
        arrival.wait()
        copy.start()
    pieces = store_sem.shape[0]
    depth = ranks // pieces
    stores = []
    for p in range(pieces):
        rows = pl.ds(p * depth, depth)
        piece = wide_ref[pl.ds(p * depth * count, depth * count), :].astype(jnp.bfloat16)
        basis_ref[rows] = piece.reshape(depth, count, nx)
        stores.append(pltpu.make_async_copy(basis_ref.at[rows], basis_out.at[rows], store_sem.at[p]))
        stores[-1].start()
    for copy in passes + stores:
        copy.wait()


def local(velocity, basis_old, strength, snapshots):
    modes = basis_old.shape[0]
    earlier_count = snapshots.shape[0]
    ranks = modes + earlier_count + 1
    sizes = tuple(lax.axis_size(axis) for axis in ("grp", "gy", "gz"))
    n_grp, n_gy, n_gz = sizes
    n_plane = n_grp * n_gy
    comps, ny, nz, nx = velocity.shape
    count = comps * (ny // 2) * (nz // 2)
    length = count * nx
    share = ranks // n_plane
    assert share * n_plane == ranks
    f32 = jnp.float32
    dma = pltpu.SemaphoreType.DMA
    vmem = pl.BlockSpec(memory_space=pltpu.VMEM)
    hbm = pl.BlockSpec(memory_space=pltpu.HBM)
    field, level, weights, whole = pl.pallas_call(
        functools.partial(kernel, sizes, float(length * n_plane * n_gz)),
        out_shape=(
            jax.ShapeDtypeStruct(velocity.shape, f32),
            jax.ShapeDtypeStruct((ranks, ranks), f32),
            jax.ShapeDtypeStruct((ranks, ranks), jnp.bfloat16),
            jax.ShapeDtypeStruct((ranks, length), jnp.bfloat16),
        ),
        in_specs=[
            hbm,
            hbm,
            hbm,
            hbm,
        ],
        out_specs=(hbm, vmem, vmem, hbm),
        scratch_shapes=[
            pltpu.VMEM(velocity.shape, f32),
            pltpu.VMEM((ranks, length), jnp.bfloat16),
            dma((2,)),
            pltpu.VMEM(velocity.shape, f32),
            pltpu.SMEM((modes,), f32),
            pltpu.VMEM((modes, count, nx), jnp.bfloat16),
            pltpu.VMEM((earlier_count, count, nx), jnp.bfloat16),
            pltpu.VMEM((ranks * count, nx), f32),
            dma((4,)),
            pltpu.VMEM((STAGES,) + velocity.shape, f32),
            pltpu.VMEM((STAGES, 2, comps, ny, nx), f32),
            pltpu.VMEM((STAGES, nz, nx), f32),
            pltpu.VMEM((STAGES, 2, comps, nz, nx), f32),
            pltpu.VMEM((STAGES, 2, comps, ny, nx), f32),
            pltpu.VMEM((STAGES, 2, nz, nx), f32),
            pltpu.VMEM((n_plane, share, ranks), f32),
            pltpu.VMEM((share, ranks), f32),
            pltpu.VMEM((n_plane, share, ranks), f32),
            pltpu.VMEM((n_gz, share, ranks), f32),
            pltpu.VMEM((n_plane, share, ranks), f32),
            pltpu.VMEM((8, ranks), f32),
            pltpu.VMEM((n_plane, 8, ranks), f32),
            pltpu.VMEM((8, ranks), f32),
            pltpu.VMEM((n_gz, 8, ranks), f32),
            dma((STAGES, 2)), dma((STAGES, 2)),
            dma((STAGES, 2)), dma((STAGES, 2)),
            dma((STAGES, 2)), dma((STAGES, 2)),
            dma((n_plane,)), dma((n_plane,)),
            dma((n_gz,)), dma((n_gz,)),
            dma((n_plane,)), dma((n_plane,)),
            dma((n_plane,)), dma((n_plane,)),
            dma((n_gz,)), dma((n_gz,)),
        ],
        compiler_params=pltpu.CompilerParams(
            collective_id=0, has_side_effects=True, vmem_limit_bytes=56 * 1024 * 1024
        ),
    )(velocity, strength, basis_old.reshape(modes, count, nx), snapshots.reshape(earlier_count, count, nx))
    field, level, basis_new = pl.pallas_call(
        rotate,
        out_shape=(
            jax.ShapeDtypeStruct(velocity.shape, f32),
            jax.ShapeDtypeStruct((ranks, ranks), f32),
            jax.ShapeDtypeStruct((ranks, count, nx), jnp.bfloat16),
        ),
        in_specs=[hbm] * 4,
        out_specs=(hbm,) * 3,
        scratch_shapes=[
            pltpu.VMEM(velocity.shape, f32),
            pltpu.VMEM((ranks, ranks), f32),
            pltpu.VMEM((ranks, ranks), jnp.bfloat16),
            pltpu.VMEM((ranks, length), jnp.bfloat16),
            pltpu.VMEM((ranks * count, nx), f32),
            pltpu.VMEM((ranks, count, nx), jnp.bfloat16),
            dma((4,)),
            dma((5,)),
            dma((4,)),
        ],
        compiler_params=pltpu.CompilerParams(vmem_limit_bytes=56 * 1024 * 1024),
    )(field, level, weights, whole)
    basis_new = basis_new.reshape(ranks, comps, ny // 2, nz // 2, nx)
    return (field, basis_new, level)


def solution(mesh):
    placed = (
        P(None, "gy", "gz", "grp"),
        P(None, None, "gy", "gz", "grp"),
        P(),
        P(None, None, "gy", "gz", "grp"),
    )
    return jax.shard_map(
        local,
        mesh=mesh,
        in_specs=placed,
        out_specs=(P(None, "gy", "gz", "grp"), P(None, None, "gy", "gz", "grp"), P()),
        check_vma=False,
    )
```

```python
import functools

import jax
import jax.numpy as jnp
from jax import lax
from jax.experimental import pallas as pl
from jax.experimental.pallas import tpu as pltpu
from jax.sharding import PartitionSpec as P

NS_ITERS = 8
STAGES = 6
DIRECT_LIMIT = 64
MESH = pl.DeviceIdType.MESH

time_step = 0.1
viscosity = 0.05


def each(count, body):
    if count <= 32:
        for i in range(count):
            body(i)
    else:
        lax.fori_loop(0, count, lambda i, carry: (body(i), carry)[1], 0)


def kernel(
    sizes, rows_total, v_hbm, strength_hbm, old_hbm, snap_hbm,
    field_hbm, level_ref, weights_ref, whole_hbm,
    field_ref, earlier_ref, store_sem,
    v_ref, strength_ref, old_ref, snap_ref, wide_ref, load_sem,
    stage, zsend, xsend, yrecv, zrecv, xrecv,
    gram_ref, part_ref, plane_ref, line_ref, full_ref,
    cross_send, cross_plane, cross_mid, cross_line,
    ysend_sem, yrecv_sem, zsend_sem, zrecv_sem, xsend_sem, xrecv_sem,
    asend_sem, arecv_sem, bsend_sem, brecv_sem, csend_sem, crecv_sem,
    dsend_sem, drecv_sem, esend_sem, erecv_sem,
):
    n_grp, n_gy, n_gz = sizes
    grp, gy, gz = lax.axis_index("grp"), lax.axis_index("gy"), lax.axis_index("gz")
    n_plane = n_grp * n_gy
    me = grp * n_gy + gy
    comps, ny, nz, nx = v_ref.shape
    ranks = earlier_ref.shape[0]
    lines = comps * ny

    def plane_id(offset):
        peer = lax.rem(me + offset, n_plane)
        return peer, {"grp": peer // n_gy, "gy": lax.rem(peer, n_gy)}

    everyone = n_plane * n_gz
    direct = everyone <= DIRECT_LIMIT
    my_place = me * n_gz + gz

    def any_id(offset):
        peer = lax.rem(my_place + offset, everyone)
        plane = peer // n_gz
        target = {"grp": plane // n_gy, "gy": lax.rem(plane, n_gy), "gz": lax.rem(peer, n_gz)}
        return peer, target

    def line_id(offset):
        peer = lax.rem(gz + offset, n_gz)
        return peer, {"gz": peer}

    y_up, y_down = {"gy": lax.rem(gy + 1, n_gy)}, {"gy": lax.rem(gy + n_gy - 1, n_gy)}
    z_up, z_down = {"gz": lax.rem(gz + 1, n_gz)}, {"gz": lax.rem(gz + n_gz - 1, n_gz)}
    x_up, x_down = {"grp": lax.rem(grp + 1, n_grp)}, {"grp": lax.rem(grp + n_grp - 1, n_grp)}
    x_ways = 1 if n_grp == 2 else 2

    loads = [
        pltpu.make_async_copy(v_hbm, v_ref, load_sem.at[2]),
        pltpu.make_async_copy(strength_hbm, strength_ref, load_sem.at[3]),
        pltpu.make_async_copy(old_hbm, old_ref, load_sem.at[0]),
        pltpu.make_async_copy(snap_hbm, snap_ref, load_sem.at[1]),
    ]
    for load in loads:
        load.start()
    barrier = pltpu.get_barrier_semaphore()

    def greet_plane(i):
        pl.semaphore_signal(barrier, inc=1, device_id=plane_id(i + 1)[1], device_id_type=MESH)

    def greet_line(i):
        pl.semaphore_signal(barrier, inc=1, device_id=line_id(i + 1)[1], device_id_type=MESH)

    def greet_any(i):
        pl.semaphore_signal(barrier, inc=1, device_id=any_id(i + 1)[1], device_id_type=MESH)

    if direct:
        each(everyone - 1, greet_any)
        greeted = everyone - 1
    else:
        each(n_plane - 1, greet_plane)
        each(n_gz - 1, greet_line)
        greeted = n_plane + n_gz - 2

    def remote(src, dst, send_sem, recv_sem, target):
        return pltpu.make_async_remote_copy(
            src_ref=src, dst_ref=dst, send_sem=send_sem, recv_sem=recv_sem,
            device_id=target, device_id_type=MESH,
        )

    def halo_copies(s):
        copies = [
            remote(stage.at[s, :, ny - 1], yrecv.at[s, 0], ysend_sem.at[s, 0], yrecv_sem.at[s, 0], y_up),
            remote(stage.at[s, :, 0], yrecv.at[s, 1], ysend_sem.at[s, 1], yrecv_sem.at[s, 1], y_down),
            remote(zsend.at[s, 0], zrecv.at[s, 0], zsend_sem.at[s, 0], zrecv_sem.at[s, 0], z_up),
            remote(zsend.at[s, 1], zrecv.at[s, 1], zsend_sem.at[s, 1], zrecv_sem.at[s, 1], z_down),
            remote(xsend.at[s], xrecv.at[s, 0], xsend_sem.at[s, 0], xrecv_sem.at[s, 0], x_up),
        ]
        if x_ways == 2:
            copies.append(
                remote(xsend.at[s], xrecv.at[s, 1], xsend_sem.at[s, 1], xrecv_sem.at[s, 1], x_down)
            )
        return copies

    lane = lax.broadcasted_iota(jnp.int32, (lines, nz, nx), 2)
    line = lax.broadcasted_iota(jnp.int32, (lines, nz, nx), 0)
    row = lax.broadcasted_iota(jnp.int32, (lines, nz, nx), 1)
    low_lane = lane == line
    high_lane = lane == line + nx // 2

    def send(s, f):
        copies = halo_copies(s)
        flat = f.reshape(lines, nz, nx)

        def pack_x():
            packed = jnp.where(low_lane, flat[:, :, 0:1], 0.0)
            packed = jnp.where(high_lane, flat[:, :, nx - 1 : nx], packed)
            xsend[s] = jnp.sum(packed, axis=0)

        zsend[s, 0] = f[:, :, nz - 1, :]
        zsend[s, 1] = f[:, :, 0, :]
        if s == 0:
            stage[s] = f
            pack_x()
            pl.semaphore_wait(barrier, greeted)
        for copy in copies[2:4]:
            copy.start()
        if s > 0:
            stage[s] = f
        for copy in copies[:2]:
            copy.start()
        if s > 0:
            pack_x()
        for copy in copies[4:]:
            copy.start()
        return copies

    def stepped(s, f, copies):
        flat = f.reshape(lines, nz, nx)
        left, right = pltpu.roll(flat, 1, 2), pltpu.roll(flat, nx - 1, 2)
        below, above = pltpu.roll(flat, 1, 1), pltpu.roll(flat, nz - 1, 1)
        for copy in copies[:2]:
            copy.wait_recv()
        bottom = jnp.where(gy == 0, 0.0, yrecv[s, 0])
        upper = jnp.where(gy == n_gy - 1, 0.0, yrecv[s, 1])
        y_minus = jnp.concatenate([bottom[:, None], f[:, :-1]], axis=1)
        y_plus = jnp.concatenate([f[:, 1:], upper[:, None]], axis=1)
        carried = f[1][None] * (y_plus - y_minus) * 0.5
        spread = y_plus + y_minus - 6.0 * f
        for copy in copies[4:]:
            copy.wait_recv()
        from_left, from_right = xrecv[s, 0], xrecv[s, x_ways - 1]
        x_low = jnp.sum(jnp.where(high_lane, from_left[None], 0.0), axis=2, keepdims=True)
        x_high = jnp.sum(jnp.where(low_lane, from_right[None], 0.0), axis=2, keepdims=True)
        x_minus = jnp.where(lane == 0, x_low, left).reshape(f.shape)
        x_plus = jnp.where(lane == nx - 1, x_high, right).reshape(f.shape)
        carried = carried + f[0][None] * (x_plus - x_minus) * 0.5
        spread = spread + (x_plus + x_minus)
        for copy in copies[2:4]:
            copy.wait_recv()
        z_low = zrecv[s, 0].reshape(lines, 1, nx)
        z_high = zrecv[s, 1].reshape(lines, 1, nx)
        z_minus = jnp.where(row == 0, z_low, below).reshape(f.shape)
        z_plus = jnp.where(row == nz - 1, z_high, above).reshape(f.shape)
        carried = carried + f[2][None] * (z_plus - z_minus) * 0.5
        spread = spread + (z_plus + z_minus)
        return f + time_step * (viscosity * spread - carried)

    def scatter_copy(i):
        peer, target = plane_id(i + 1)
        return remote(
            gram_ref.at[peer], plane_ref.at[me], asend_sem.at[i], arecv_sem.at[me], target
        )

    def line_copy(i):
        _, target = line_id(i + 1)
        return remote(part_ref, line_ref.at[gz], bsend_sem.at[i], brecv_sem.at[gz], target)

    def gather_copy(i):
        _, target = plane_id(i + 1)
        return remote(
            full_ref.at[me], full_ref.at[me], csend_sem.at[i], crecv_sem.at[me], target
        )

    def cross_plane_copy(i):
        _, target = plane_id(i + 1)
        return remote(cross_send, cross_plane.at[me], dsend_sem.at[i], drecv_sem.at[me], target)

    def cross_line_copy(i):
        _, target = line_id(i + 1)
        return remote(cross_mid, cross_line.at[gz], esend_sem.at[i], erecv_sem.at[gz], target)

    def cross_any_copy(i):
        _, target = any_id(i + 1)
        return remote(
            cross_send, cross_plane.at[my_place], dsend_sem.at[i], drecv_sem.at[my_place], target
        )

    def wait_any(buffer, sem):
        def body(i):
            peer, target = any_id(i + 1)
            remote(buffer.at[peer], buffer.at[peer], sem.at[peer], sem.at[peer], target).wait_recv()

        each(everyone - 1, body)

    def wait_plane(buffer, sem):
        def body(i):
            peer, target = plane_id(i + 1)
            remote(buffer.at[peer], buffer.at[peer], sem.at[peer], sem.at[peer], target).wait_recv()

        each(n_plane - 1, body)

    def wait_line(buffer, sem):
        def body(i):
            peer, target = line_id(i + 1)
            remote(buffer.at[peer], buffer.at[peer], sem.at[peer], sem.at[peer], target).wait_recv()

        each(n_gz - 1, body)

    modes, count = old_ref.shape[0], old_ref.shape[1]

    def flatten_old():
        for load in loads[1:]:
            load.wait()

        def scale_row(r, carry):
            wide_ref[pl.ds(r * count, count), :] = strength_ref[r] * old_ref[r].astype(jnp.float32)
            return carry

        lax.fori_loop(0, modes, scale_row, 0, unroll=8)

    def flatten_snapshots():
        def copy_row(r, carry):
            wide_ref[pl.ds((r + modes) * count, count), :] = snap_ref[r].astype(jnp.float32)
            return carry

        lax.fori_loop(0, snap_ref.shape[0], copy_row, 0, unroll=7)
        wide_ref[pl.ds((ranks - 1) * count, count), :] = jnp.zeros((count, nx), jnp.float32)
        take_columns(0, count // 2)

    def take_columns(first, stop):
        for b in range(first, stop):
            column = wide_ref[pl.ds(b, ranks, stride=count), :]
            earlier_ref[:, b * nx : (b + 1) * nx] = column.astype(jnp.bfloat16)

    def begin_gram():
        take_columns(count // 2, count)
        earlier = earlier_ref[...]
        gram = lax.dot_general(
            earlier, earlier, (((1,), (1,)), ((), ())), preferred_element_type=jnp.float32
        )
        gram_ref[...] = gram.reshape(gram_ref.shape)
        plane_ref[me] = gram_ref[me]
        each(n_plane - 1, lambda i: scatter_copy(i).start())

    def add_plane():
        wait_plane(plane_ref, arecv_sem)
        part = jnp.sum(plane_ref[...], axis=0)
        part_ref[...] = part
        line_ref[gz] = part
        each(n_gz - 1, lambda i: line_copy(i).start())

    def add_line():
        wait_line(line_ref, brecv_sem)
        full_ref[me] = jnp.sum(line_ref[...], axis=0)
        each(n_plane - 1, lambda i: gather_copy(i).start())

    between = {0: flatten_old, 1: flatten_snapshots, 2: begin_gram, 3: add_plane, 4: add_line}
    loads[0].wait()
    base = v_ref[...]
    f = base
    for s in range(STAGES):
        copies = send(s, f)
        if s in between:
            between[s]()
        moved = stepped(s, f, copies)
        if s % 3 == 0:
            f = moved
        elif s % 3 == 1:
            f = 0.75 * base + 0.25 * moved
        else:
            f = base / 3.0 + 2.0 / 3.0 * moved
            base = f
    field_ref[...] = f
    field_store = pltpu.make_async_copy(field_ref, field_hbm, store_sem.at[0])
    field_store.start()

    blocks = [(c, y, z) for c in range(comps) for y in range(0, ny, 2) for z in range(0, nz, 2)]

    def newest_block(b):
        c, y, z = blocks[b]
        return field_ref[c, y, pl.ds(z, 1), :].astype(jnp.bfloat16).astype(jnp.float32)

    total = jnp.zeros((ranks, nx), jnp.float32)
    own = jnp.zeros((1, nx), jnp.float32)
    for b in range(len(blocks)):
        newest = newest_block(b)
        total = total + earlier_ref[:, b * nx : (b + 1) * nx].astype(jnp.float32) * newest
        own = own + newest * newest
    square_row = lax.broadcasted_iota(jnp.int32, (ranks, ranks), 0)
    square_col = lax.broadcasted_iota(jnp.int32, (ranks, ranks), 1)
    total = jnp.where(lax.broadcasted_iota(jnp.int32, (ranks, nx), 0) == ranks - 1, own, total)
    cross = jnp.sum(total.T, axis=0, keepdims=True)
    cross_send[...] = cross
    if direct:
        cross_plane[my_place] = cross
        each(everyone - 1, lambda i: cross_any_copy(i).start())
    else:
        cross_plane[me] = cross
        each(n_plane - 1, lambda i: cross_plane_copy(i).start())
    tail = slice(ranks - 16, ranks)
    last = lax.broadcasted_iota(jnp.int32, (16, nx), 0) == 15
    for b in range(len(blocks)):
        columns = slice(b * nx, (b + 1) * nx)
        rows = earlier_ref[tail, columns].astype(jnp.float32)
        earlier_ref[tail, columns] = jnp.where(last, newest_block(b), rows).astype(jnp.bfloat16)
    whole_store = pltpu.make_async_copy(earlier_ref, whole_hbm, store_sem.at[1])
    whole_store.start()
    wait_plane(full_ref, crecv_sem)
    if direct:
        wait_any(cross_plane, drecv_sem)
        cross = jnp.sum(cross_plane[...], axis=0)
    else:
        wait_plane(cross_plane, drecv_sem)
        cross_mid[...] = jnp.sum(cross_plane[...], axis=0)
        cross_line[gz] = cross_mid[...]
        each(n_gz - 1, lambda i: cross_line_copy(i).start())
        wait_line(cross_line, erecv_sem)
        cross = jnp.sum(cross_line[...], axis=0)
    cross = jnp.broadcast_to(cross, (ranks, ranks))

    gram = full_ref[...].reshape(ranks, ranks)
    gram = jnp.where(square_col == ranks - 1, cross.T, gram)
    gram = jnp.where(square_row == ranks - 1, cross, gram)
    scale = jnp.sqrt(jnp.sum(gram * gram, keepdims=True))
    level = gram / scale
    ident = jnp.where(square_row == square_col, 1.0, 0.0)

    def split(a):
        coarse = a.astype(jnp.bfloat16)
        return coarse, (a - coarse.astype(jnp.float32)).astype(jnp.bfloat16)

    def dot(left, right):
        terms = jnp.concatenate(right, axis=1)
        both = jnp.dot(
            jnp.concatenate(left, axis=1),
            jnp.concatenate([terms, terms], axis=0),
            preferred_element_type=jnp.float32,
        )
        return both[:, :ranks] + both[:, ranks:]

    inverse, inverse_split = ident, None
    for repeat in range(NS_ITERS):
        level_split = split(level)
        product = level if repeat == 0 else dot(inverse_split, level_split)
        product_split = split(product)
        moved = product if repeat == 0 else dot(product_split, inverse_split)
        inverse = 1.5 * inverse - 0.5 * moved
        level = 1.5 * level - 0.5 * dot(level_split, product_split)
        inverse_split = split(inverse)
    level_ref[...] = level
    factor = jnp.sqrt(jnp.full((1, 1), rows_total, jnp.float32)) / jnp.sqrt(scale)
    weights = (inverse * factor).astype(jnp.bfloat16)
    weights_ref[...] = weights

    field_store.wait()
    whole_store.wait()
    for s in range(STAGES):
        for copy in halo_copies(s):
            copy.wait_send()
    each(n_plane - 1, lambda i: scatter_copy(i).wait_send())
    each(n_gz - 1, lambda i: line_copy(i).wait_send())
    each(n_plane - 1, lambda i: gather_copy(i).wait_send())
    if direct:
        each(everyone - 1, lambda i: cross_any_copy(i).wait_send())
    else:
        each(n_plane - 1, lambda i: cross_plane_copy(i).wait_send())
        each(n_gz - 1, lambda i: cross_line_copy(i).wait_send())


def rotate(
    field_in, level_in, weights_in, whole_in, field_out, level_out, basis_out,
    field_ref, level_ref, weights_ref, whole_ref, wide_ref, basis_ref, pass_sem, load_sem, store_sem,
):
    ranks, count, nx = basis_ref.shape
    parts = load_sem.shape[0] - 1
    width = count // parts * nx
    loads = [pltpu.make_async_copy(weights_in, weights_ref, load_sem.at[parts])]
    for p in range(parts):
        columns = (slice(None), pl.ds(p * width, width))
        loads.append(pltpu.make_async_copy(whole_in.at[columns], whole_ref.at[columns], load_sem.at[p]))
    arrivals = [
        pltpu.make_async_copy(field_in, field_ref, pass_sem.at[0]),
        pltpu.make_async_copy(level_in, level_ref, pass_sem.at[1]),
    ]
    passes = [
        pltpu.make_async_copy(field_ref, field_out, pass_sem.at[2]),
        pltpu.make_async_copy(level_ref, level_out, pass_sem.at[3]),
    ]
    for copy in loads + arrivals:
        copy.start()
    loads[0].wait()
    weights = weights_ref[...]
    for p in range(parts):
        loads[p + 1].wait()
        for b in range(p * count // parts, (p + 1) * count // parts, 2):
            pair = jnp.dot(
                weights, whole_ref[:, b * nx : (b + 2) * nx], preferred_element_type=jnp.float32
            )
            wide_ref[pl.ds(b, ranks, stride=count), :] = pair[:, :nx]
            wide_ref[pl.ds(b + 1, ranks, stride=count), :] = pair[:, nx:]
    for arrival, copy in zip(arrivals, passes):
        arrival.wait()
        copy.start()
    pieces = store_sem.shape[0]
    depth = ranks // pieces
    stores = []
    for p in range(pieces):
        rows = pl.ds(p * depth, depth)
        piece = wide_ref[pl.ds(p * depth * count, depth * count), :].astype(jnp.bfloat16)
        basis_ref[rows] = piece.reshape(depth, count, nx)
        stores.append(pltpu.make_async_copy(basis_ref.at[rows], basis_out.at[rows], store_sem.at[p]))
        stores[-1].start()
    for copy in passes + stores:
        copy.wait()


def local(velocity, basis_old, strength, snapshots):
    modes = basis_old.shape[0]
    earlier_count = snapshots.shape[0]
    ranks = modes + earlier_count + 1
    sizes = tuple(lax.axis_size(axis) for axis in ("grp", "gy", "gz"))
    n_grp, n_gy, n_gz = sizes
    n_plane = n_grp * n_gy
    comps, ny, nz, nx = velocity.shape
    count = comps * (ny // 2) * (nz // 2)
    length = count * nx
    share = ranks // n_plane
    assert share * n_plane == ranks
    everyone = n_plane * n_gz
    senders = everyone if everyone <= DIRECT_LIMIT else n_plane
    f32 = jnp.float32
    dma = pltpu.SemaphoreType.DMA
    vmem = pl.BlockSpec(memory_space=pltpu.VMEM)
    hbm = pl.BlockSpec(memory_space=pltpu.HBM)
    field, level, weights, whole = pl.pallas_call(
        functools.partial(kernel, sizes, float(length * n_plane * n_gz)),
        out_shape=(
            jax.ShapeDtypeStruct(velocity.shape, f32),
            jax.ShapeDtypeStruct((ranks, ranks), f32),
            jax.ShapeDtypeStruct((ranks, ranks), jnp.bfloat16),
            jax.ShapeDtypeStruct((ranks, length), jnp.bfloat16),
        ),
        in_specs=[
            hbm,
            hbm,
            hbm,
            hbm,
        ],
        out_specs=(hbm, vmem, vmem, hbm),
        scratch_shapes=[
            pltpu.VMEM(velocity.shape, f32),
            pltpu.VMEM((ranks, length), jnp.bfloat16),
            dma((2,)),
            pltpu.VMEM(velocity.shape, f32),
            pltpu.SMEM((modes,), f32),
            pltpu.VMEM((modes, count, nx), jnp.bfloat16),
            pltpu.VMEM((earlier_count, count, nx), jnp.bfloat16),
            pltpu.VMEM((ranks * count, nx), f32),
            dma((4,)),
            pltpu.VMEM((STAGES,) + velocity.shape, f32),
            pltpu.VMEM((STAGES, 2, comps, ny, nx), f32),
            pltpu.VMEM((STAGES, nz, nx), f32),
            pltpu.VMEM((STAGES, 2, comps, nz, nx), f32),
            pltpu.VMEM((STAGES, 2, comps, ny, nx), f32),
            pltpu.VMEM((STAGES, 2, nz, nx), f32),
            pltpu.VMEM((n_plane, share, ranks), f32),
            pltpu.VMEM((share, ranks), f32),
            pltpu.VMEM((n_plane, share, ranks), f32),
            pltpu.VMEM((n_gz, share, ranks), f32),
            pltpu.VMEM((n_plane, share, ranks), f32),
            pltpu.VMEM((1, ranks), f32),
            pltpu.VMEM((senders, 1, ranks), f32),
            pltpu.VMEM((1, ranks), f32),
            pltpu.VMEM((n_gz, 1, ranks), f32),
            dma((STAGES, 2)), dma((STAGES, 2)),
            dma((STAGES, 2)), dma((STAGES, 2)),
            dma((STAGES, 2)), dma((STAGES, 2)),
            dma((n_plane,)), dma((n_plane,)),
            dma((n_gz,)), dma((n_gz,)),
            dma((n_plane,)), dma((n_plane,)),
            dma((senders,)), dma((senders,)),
            dma((n_gz,)), dma((n_gz,)),
        ],
        compiler_params=pltpu.CompilerParams(
            collective_id=0, has_side_effects=True, vmem_limit_bytes=56 * 1024 * 1024
        ),
    )(velocity, strength, basis_old.reshape(modes, count, nx), snapshots.reshape(earlier_count, count, nx))
    field, level, basis_new = pl.pallas_call(
        rotate,
        out_shape=(
            jax.ShapeDtypeStruct(velocity.shape, f32),
            jax.ShapeDtypeStruct((ranks, ranks), f32),
            jax.ShapeDtypeStruct((ranks, count, nx), jnp.bfloat16),
        ),
        in_specs=[hbm] * 4,
        out_specs=(hbm,) * 3,
        scratch_shapes=[
            pltpu.VMEM(velocity.shape, f32),
            pltpu.VMEM((ranks, ranks), f32),
            pltpu.VMEM((ranks, ranks), jnp.bfloat16),
            pltpu.VMEM((ranks, length), jnp.bfloat16),
            pltpu.VMEM((ranks * count, nx), f32),
            pltpu.VMEM((ranks, count, nx), jnp.bfloat16),
            dma((4,)),
            dma((5,)),
            dma((4,)),
        ],
        compiler_params=pltpu.CompilerParams(vmem_limit_bytes=56 * 1024 * 1024),
    )(field, level, weights, whole)
    basis_new = basis_new.reshape(ranks, comps, ny // 2, nz // 2, nx)
    return (field, basis_new, level)


def solution(mesh):
    placed = (
        P(None, "gy", "gz", "grp"),
        P(None, None, "gy", "gz", "grp"),
        P(),
        P(None, None, "gy", "gz", "grp"),
    )
    return jax.shard_map(
        local,
        mesh=mesh,
        in_specs=placed,
        out_specs=(P(None, "gy", "gz", "grp"), P(None, None, "gy", "gz", "grp"), P()),
        check_vma=False,
    )
```

```python
import functools

import jax
import jax.numpy as jnp
from jax import lax
from jax.experimental import pallas as pl
from jax.experimental.pallas import tpu as pltpu
from jax.sharding import PartitionSpec as P

NS_ITERS = 8
STAGES = 6
DIRECT_LIMIT = 64
MESH = pl.DeviceIdType.MESH

time_step = 0.1
viscosity = 0.05


def each(count, body):
    if count <= 32:
        for i in range(count):
            body(i)
    else:
        lax.fori_loop(0, count, lambda i, carry: (body(i), carry)[1], 0)


def kernel(
    sizes, rows_total, v_hbm, strength_hbm, old_hbm, snap_hbm,
    field_hbm, level_ref, weights_ref, whole_hbm,
    field_ref, earlier_ref, store_sem,
    v_ref, strength_ref, old_ref, snap_ref, wide_ref, load_sem,
    rows_ref, stage, zsend, xsend, yrecv, zrecv, xrecv,
    gram_ref, part_ref, plane_ref, line_ref, full_ref,
    cross_send, cross_plane, cross_mid, cross_line,
    ysend_sem, yrecv_sem, zsend_sem, zrecv_sem, xsend_sem, xrecv_sem,
    asend_sem, arecv_sem, bsend_sem, brecv_sem, csend_sem, crecv_sem,
    dsend_sem, drecv_sem, esend_sem, erecv_sem,
):
    n_grp, n_gy, n_gz = sizes
    grp, gy, gz = lax.axis_index("grp"), lax.axis_index("gy"), lax.axis_index("gz")
    n_plane = n_grp * n_gy
    me = grp * n_gy + gy
    comps, ny, nz, nx = v_ref.shape
    ranks = earlier_ref.shape[0]
    lines = comps * ny

    def plane_id(offset):
        peer = lax.rem(me + offset, n_plane)
        return peer, {"grp": peer // n_gy, "gy": lax.rem(peer, n_gy)}

    everyone = n_plane * n_gz
    direct = everyone <= DIRECT_LIMIT
    my_place = me * n_gz + gz

    def any_id(offset):
        peer = lax.rem(my_place + offset, everyone)
        plane = peer // n_gz
        target = {"grp": plane // n_gy, "gy": lax.rem(plane, n_gy), "gz": lax.rem(peer, n_gz)}
        return peer, target

    def line_id(offset):
        peer = lax.rem(gz + offset, n_gz)
        return peer, {"gz": peer}

    y_up, y_down = {"gy": lax.rem(gy + 1, n_gy)}, {"gy": lax.rem(gy + n_gy - 1, n_gy)}
    z_up, z_down = {"gz": lax.rem(gz + 1, n_gz)}, {"gz": lax.rem(gz + n_gz - 1, n_gz)}
    x_up, x_down = {"grp": lax.rem(grp + 1, n_grp)}, {"grp": lax.rem(grp + n_grp - 1, n_grp)}
    x_ways = 1 if n_grp == 2 else 2

    loads = [
        pltpu.make_async_copy(v_hbm, v_ref, load_sem.at[2]),
        pltpu.make_async_copy(strength_hbm, strength_ref, load_sem.at[3]),
        pltpu.make_async_copy(old_hbm, old_ref, load_sem.at[0]),
        pltpu.make_async_copy(snap_hbm, snap_ref, load_sem.at[1]),
    ]
    for load in loads:
        load.start()
    barrier = pltpu.get_barrier_semaphore()

    def greet_plane(i):
        pl.semaphore_signal(barrier, inc=1, device_id=plane_id(i + 1)[1], device_id_type=MESH)

    def greet_line(i):
        pl.semaphore_signal(barrier, inc=1, device_id=line_id(i + 1)[1], device_id_type=MESH)

    def greet_any(i):
        pl.semaphore_signal(barrier, inc=1, device_id=any_id(i + 1)[1], device_id_type=MESH)

    if direct:
        each(everyone - 1, greet_any)
        greeted = everyone - 1
    else:
        each(n_plane - 1, greet_plane)
        each(n_gz - 1, greet_line)
        greeted = n_plane + n_gz - 2

    def remote(src, dst, send_sem, recv_sem, target):
        return pltpu.make_async_remote_copy(
            src_ref=src, dst_ref=dst, send_sem=send_sem, recv_sem=recv_sem,
            device_id=target, device_id_type=MESH,
        )

    def halo_copies(s):
        copies = [
            remote(stage.at[s, :, ny - 1], yrecv.at[s, 0], ysend_sem.at[s, 0], yrecv_sem.at[s, 0], y_up),
            remote(stage.at[s, :, 0], yrecv.at[s, 1], ysend_sem.at[s, 1], yrecv_sem.at[s, 1], y_down),
            remote(zsend.at[s, 0], zrecv.at[s, 0], zsend_sem.at[s, 0], zrecv_sem.at[s, 0], z_up),
            remote(zsend.at[s, 1], zrecv.at[s, 1], zsend_sem.at[s, 1], zrecv_sem.at[s, 1], z_down),
            remote(xsend.at[s], xrecv.at[s, 0], xsend_sem.at[s, 0], xrecv_sem.at[s, 0], x_up),
        ]
        if x_ways == 2:
            copies.append(
                remote(xsend.at[s], xrecv.at[s, 1], xsend_sem.at[s, 1], xrecv_sem.at[s, 1], x_down)
            )
        return copies

    lane = lax.broadcasted_iota(jnp.int32, (lines, nz, nx), 2)
    flat_lane = lax.broadcasted_iota(jnp.int32, (nz, nx), 1)
    pair = flat_lane // 2
    even = flat_lane % 2 == 0

    def send(s, f):
        copies = halo_copies(s)
        flat = f.reshape(lines, nz, nx)

        def pack_x():
            packed = jnp.zeros((nz, nx), jnp.float32)
            for k in range(lines):
                packed = jnp.where(pair == k, pltpu.roll(flat[k], 2 * k + 1, 1), packed)
            xsend[s] = packed

        rows_ref[0] = f.reshape(lines * nz, nx)
        zsend[s, 0] = rows_ref[0, pl.ds(nz - 1, lines, stride=nz), :]
        zsend[s, 1] = rows_ref[0, pl.ds(0, lines, stride=nz), :]
        if s == 0:
            stage[s] = f
            pack_x()
            pl.semaphore_wait(barrier, greeted)
        for copy in copies[2:4]:
            copy.start()
        if s > 0:
            stage[s] = f
        for copy in copies[:2]:
            copy.start()
        if s > 0:
            pack_x()
        for copy in copies[4:]:
            copy.start()
        return copies

    def stepped(s, f, copies):
        flat = f.reshape(lines, nz, nx)
        left, right = pltpu.roll(flat, 1, 2), pltpu.roll(flat, nx - 1, 2)
        rows_ref[1] = pltpu.roll(flat, 1, 1).reshape(lines * nz, nx)
        rows_ref[2] = pltpu.roll(flat, nz - 1, 1).reshape(lines * nz, nx)
        for copy in copies[:2]:
            copy.wait_recv()
        bottom = jnp.where(gy == 0, 0.0, yrecv[s, 0])
        upper = jnp.where(gy == n_gy - 1, 0.0, yrecv[s, 1])
        y_minus = jnp.concatenate([bottom[:, None], f[:, :-1]], axis=1)
        y_plus = jnp.concatenate([f[:, 1:], upper[:, None]], axis=1)
        carried = f[1][None] * (y_plus - y_minus) * 0.5
        spread = y_plus + y_minus - 6.0 * f
        for copy in copies[4:]:
            copy.wait_recv()
        from_left, from_right = xrecv[s, 0], xrecv[s, x_ways - 1]
        merged = jnp.where(even, from_left, pltpu.roll(from_right, nx - 2, 1))
        edges = jnp.stack([pltpu.roll(merged, (nx - 2 * k) % nx, 1) if k else merged for k in range(lines)])
        x_minus = jnp.where(lane == 0, edges, left).reshape(f.shape)
        x_plus = jnp.where(lane == nx - 1, edges, right).reshape(f.shape)
        carried = carried + f[0][None] * (x_plus - x_minus) * 0.5
        spread = spread + (x_plus + x_minus)
        for copy in copies[2:4]:
            copy.wait_recv()
        rows_ref[1, pl.ds(0, lines, stride=nz), :] = zrecv[s, 0]
        rows_ref[2, pl.ds(nz - 1, lines, stride=nz), :] = zrecv[s, 1]
        z_minus = rows_ref[1].reshape(f.shape)
        z_plus = rows_ref[2].reshape(f.shape)
        carried = carried + f[2][None] * (z_plus - z_minus) * 0.5
        spread = spread + (z_plus + z_minus)
        return f + time_step * (viscosity * spread - carried)

    def scatter_copy(i):
        peer, target = plane_id(i + 1)
        return remote(
            gram_ref.at[peer], plane_ref.at[me], asend_sem.at[i], arecv_sem.at[me], target
        )

    def line_copy(i):
        _, target = line_id(i + 1)
        return remote(part_ref, line_ref.at[gz], bsend_sem.at[i], brecv_sem.at[gz], target)

    def gather_copy(i):
        _, target = plane_id(i + 1)
        return remote(
            full_ref.at[me], full_ref.at[me], csend_sem.at[i], crecv_sem.at[me], target
        )

    def cross_plane_copy(i):
        _, target = plane_id(i + 1)
        return remote(cross_send, cross_plane.at[me], dsend_sem.at[i], drecv_sem.at[me], target)

    def cross_line_copy(i):
        _, target = line_id(i + 1)
        return remote(cross_mid, cross_line.at[gz], esend_sem.at[i], erecv_sem.at[gz], target)

    def cross_any_copy(i):
        _, target = any_id(i + 1)
        return remote(
            cross_send, cross_plane.at[my_place], dsend_sem.at[i], drecv_sem.at[my_place], target
        )

    def wait_any(buffer, sem):
        def body(i):
            peer, target = any_id(i + 1)
            remote(buffer.at[peer], buffer.at[peer], sem.at[peer], sem.at[peer], target).wait_recv()

        each(everyone - 1, body)

    def wait_plane(buffer, sem):
        def body(i):
            peer, target = plane_id(i + 1)
            remote(buffer.at[peer], buffer.at[peer], sem.at[peer], sem.at[peer], target).wait_recv()

        each(n_plane - 1, body)

    def wait_line(buffer, sem):
        def body(i):
            peer, target = line_id(i + 1)
            remote(buffer.at[peer], buffer.at[peer], sem.at[peer], sem.at[peer], target).wait_recv()

        each(n_gz - 1, body)

    modes, count = old_ref.shape[0], old_ref.shape[1]

    def flatten_old():
        for load in loads[1:]:
            load.wait()

        def scale_row(r, carry):
            wide_ref[pl.ds(r * count, count), :] = strength_ref[r] * old_ref[r].astype(jnp.float32)
            return carry

        lax.fori_loop(0, modes, scale_row, 0, unroll=8)

    def flatten_snapshots():
        def copy_row(r, carry):
            wide_ref[pl.ds((r + modes) * count, count), :] = snap_ref[r].astype(jnp.float32)
            return carry

        lax.fori_loop(0, snap_ref.shape[0], copy_row, 0, unroll=7)
        wide_ref[pl.ds((ranks - 1) * count, count), :] = jnp.zeros((count, nx), jnp.float32)
        take_columns(0, count // 2)

    def take_columns(first, stop):
        for b in range(first, stop):
            column = wide_ref[pl.ds(b, ranks, stride=count), :]
            earlier_ref[:, b * nx : (b + 1) * nx] = column.astype(jnp.bfloat16)

    def begin_gram():
        take_columns(count // 2, count)
        earlier = earlier_ref[...]
        gram = lax.dot_general(
            earlier, earlier, (((1,), (1,)), ((), ())), preferred_element_type=jnp.float32
        )
        gram_ref[...] = gram.reshape(gram_ref.shape)
        plane_ref[me] = gram_ref[me]
        each(n_plane - 1, lambda i: scatter_copy(i).start())

    def add_plane():
        wait_plane(plane_ref, arecv_sem)
        part = jnp.sum(plane_ref[...], axis=0)
        part_ref[...] = part
        line_ref[gz] = part
        each(n_gz - 1, lambda i: line_copy(i).start())

    def add_line():
        wait_line(line_ref, brecv_sem)
        full_ref[me] = jnp.sum(line_ref[...], axis=0)
        each(n_plane - 1, lambda i: gather_copy(i).start())

    between = {0: flatten_old, 1: flatten_snapshots, 2: begin_gram, 3: add_plane, 4: add_line}
    loads[0].wait()
    base = v_ref[...]
    f = base
    for s in range(STAGES):
        copies = send(s, f)
        if s in between:
            between[s]()
        moved = stepped(s, f, copies)
        if s % 3 == 0:
            f = moved
        elif s % 3 == 1:
            f = 0.75 * base + 0.25 * moved
        else:
            f = base / 3.0 + 2.0 / 3.0 * moved
            base = f
    field_ref[...] = f
    field_store = pltpu.make_async_copy(field_ref, field_hbm, store_sem.at[0])
    field_store.start()

    blocks = [(c, y, z) for c in range(comps) for y in range(0, ny, 2) for z in range(0, nz, 2)]

    def newest_block(b):
        c, y, z = blocks[b]
        return field_ref[c, y, pl.ds(z, 1), :].astype(jnp.bfloat16).astype(jnp.float32)

    total = jnp.zeros((ranks, nx), jnp.float32)
    own = jnp.zeros((1, nx), jnp.float32)
    for b in range(len(blocks)):
        newest = newest_block(b)
        total = total + earlier_ref[:, b * nx : (b + 1) * nx].astype(jnp.float32) * newest
        own = own + newest * newest
    square_row = lax.broadcasted_iota(jnp.int32, (ranks, ranks), 0)
    square_col = lax.broadcasted_iota(jnp.int32, (ranks, ranks), 1)
    total = jnp.where(lax.broadcasted_iota(jnp.int32, (ranks, nx), 0) == ranks - 1, own, total)
    cross = jnp.sum(total.T, axis=0, keepdims=True)
    cross_send[...] = cross
    if direct:
        cross_plane[my_place] = cross
        each(everyone - 1, lambda i: cross_any_copy(i).start())
    else:
        cross_plane[me] = cross
        each(n_plane - 1, lambda i: cross_plane_copy(i).start())
    tail = slice(ranks - 16, ranks)
    last = lax.broadcasted_iota(jnp.int32, (16, nx), 0) == 15
    for b in range(len(blocks)):
        columns = slice(b * nx, (b + 1) * nx)
        rows = earlier_ref[tail, columns].astype(jnp.float32)
        earlier_ref[tail, columns] = jnp.where(last, newest_block(b), rows).astype(jnp.bfloat16)
    whole_store = pltpu.make_async_copy(earlier_ref, whole_hbm, store_sem.at[1])
    whole_store.start()
    wait_plane(full_ref, crecv_sem)
    if direct:
        wait_any(cross_plane, drecv_sem)
        cross = jnp.sum(cross_plane[...], axis=0)
    else:
        wait_plane(cross_plane, drecv_sem)
        cross_mid[...] = jnp.sum(cross_plane[...], axis=0)
        cross_line[gz] = cross_mid[...]
        each(n_gz - 1, lambda i: cross_line_copy(i).start())
        wait_line(cross_line, erecv_sem)
        cross = jnp.sum(cross_line[...], axis=0)
    cross = jnp.broadcast_to(cross, (ranks, ranks))

    gram = full_ref[...].reshape(ranks, ranks)
    gram = jnp.where(square_col == ranks - 1, cross.T, gram)
    gram = jnp.where(square_row == ranks - 1, cross, gram)
    scale = jnp.sqrt(jnp.sum(gram * gram, keepdims=True))
    level = gram / scale
    ident = jnp.where(square_row == square_col, 1.0, 0.0)

    def split(a):
        coarse = a.astype(jnp.bfloat16)
        return coarse, (a - coarse.astype(jnp.float32)).astype(jnp.bfloat16)

    def dot(left, right):
        terms = jnp.concatenate(right, axis=1)
        both = jnp.dot(
            jnp.concatenate(left, axis=1),
            jnp.concatenate([terms, terms], axis=0),
            preferred_element_type=jnp.float32,
        )
        return both[:, :ranks] + both[:, ranks:]

    inverse, inverse_split = ident, None
    for repeat in range(NS_ITERS):
        level_split = split(level)
        product = level if repeat == 0 else dot(inverse_split, level_split)
        product_split = split(product)
        moved = product if repeat == 0 else dot(product_split, inverse_split)
        inverse = 1.5 * inverse - 0.5 * moved
        level = 1.5 * level - 0.5 * dot(level_split, product_split)
        inverse_split = split(inverse)
    level_ref[...] = level
    factor = jnp.sqrt(jnp.full((1, 1), rows_total, jnp.float32)) / jnp.sqrt(scale)
    weights = (inverse * factor).astype(jnp.bfloat16)
    weights_ref[...] = weights

    field_store.wait()
    whole_store.wait()
    for s in range(STAGES):
        for copy in halo_copies(s):
            copy.wait_send()
    each(n_plane - 1, lambda i: scatter_copy(i).wait_send())
    each(n_gz - 1, lambda i: line_copy(i).wait_send())
    each(n_plane - 1, lambda i: gather_copy(i).wait_send())
    if direct:
        each(everyone - 1, lambda i: cross_any_copy(i).wait_send())
    else:
        each(n_plane - 1, lambda i: cross_plane_copy(i).wait_send())
        each(n_gz - 1, lambda i: cross_line_copy(i).wait_send())


def rotate(
    field_in, level_in, weights_in, whole_in, field_out, level_out, basis_out,
    field_ref, level_ref, weights_ref, whole_ref, wide_ref, basis_ref, pass_sem, load_sem, store_sem,
):
    ranks, count, nx = basis_ref.shape
    parts = load_sem.shape[0] - 1
    width = count // parts * nx
    loads = [pltpu.make_async_copy(weights_in, weights_ref, load_sem.at[parts])]
    for p in range(parts):
        columns = (slice(None), pl.ds(p * width, width))
        loads.append(pltpu.make_async_copy(whole_in.at[columns], whole_ref.at[columns], load_sem.at[p]))
    arrivals = [
        pltpu.make_async_copy(field_in, field_ref, pass_sem.at[0]),
        pltpu.make_async_copy(level_in, level_ref, pass_sem.at[1]),
    ]
    passes = [
        pltpu.make_async_copy(field_ref, field_out, pass_sem.at[2]),
        pltpu.make_async_copy(level_ref, level_out, pass_sem.at[3]),
    ]
    for copy in loads + arrivals:
        copy.start()
    loads[0].wait()
    weights = weights_ref[...]
    for p in range(parts):
        loads[p + 1].wait()
        for b in range(p * count // parts, (p + 1) * count // parts, 2):
            pair = jnp.dot(
                weights, whole_ref[:, b * nx : (b + 2) * nx], preferred_element_type=jnp.float32
            )
            wide_ref[pl.ds(b, ranks, stride=count), :] = pair[:, :nx]
            wide_ref[pl.ds(b + 1, ranks, stride=count), :] = pair[:, nx:]
    for arrival, copy in zip(arrivals, passes):
        arrival.wait()
        copy.start()
    pieces = store_sem.shape[0]
    depth = ranks // pieces
    stores = []
    for p in range(pieces):
        rows = pl.ds(p * depth, depth)
        piece = wide_ref[pl.ds(p * depth * count, depth * count), :].astype(jnp.bfloat16)
        basis_ref[rows] = piece.reshape(depth, count, nx)
        stores.append(pltpu.make_async_copy(basis_ref.at[rows], basis_out.at[rows], store_sem.at[p]))
        stores[-1].start()
    for copy in passes + stores:
        copy.wait()


def local(velocity, basis_old, strength, snapshots):
    modes = basis_old.shape[0]
    earlier_count = snapshots.shape[0]
    ranks = modes + earlier_count + 1
    sizes = tuple(lax.axis_size(axis) for axis in ("grp", "gy", "gz"))
    n_grp, n_gy, n_gz = sizes
    n_plane = n_grp * n_gy
    comps, ny, nz, nx = velocity.shape
    count = comps * (ny // 2) * (nz // 2)
    length = count * nx
    share = ranks // n_plane
    assert share * n_plane == ranks
    everyone = n_plane * n_gz
    senders = everyone if everyone <= DIRECT_LIMIT else n_plane
    f32 = jnp.float32
    dma = pltpu.SemaphoreType.DMA
    vmem = pl.BlockSpec(memory_space=pltpu.VMEM)
    hbm = pl.BlockSpec(memory_space=pltpu.HBM)
    field, level, weights, whole = pl.pallas_call(
        functools.partial(kernel, sizes, float(length * n_plane * n_gz)),
        out_shape=(
            jax.ShapeDtypeStruct(velocity.shape, f32),
            jax.ShapeDtypeStruct((ranks, ranks), f32),
            jax.ShapeDtypeStruct((ranks, ranks), jnp.bfloat16),
            jax.ShapeDtypeStruct((ranks, length), jnp.bfloat16),
        ),
        in_specs=[
            hbm,
            hbm,
            hbm,
            hbm,
        ],
        out_specs=(hbm, vmem, vmem, hbm),
        scratch_shapes=[
            pltpu.VMEM(velocity.shape, f32),
            pltpu.VMEM((ranks, length), jnp.bfloat16),
            dma((2,)),
            pltpu.VMEM(velocity.shape, f32),
            pltpu.SMEM((modes,), f32),
            pltpu.VMEM((modes, count, nx), jnp.bfloat16),
            pltpu.VMEM((earlier_count, count, nx), jnp.bfloat16),
            pltpu.VMEM((ranks * count, nx), f32),
            dma((4,)),
            pltpu.VMEM((3, comps * ny * nz, nx), f32),
            pltpu.VMEM((STAGES,) + velocity.shape, f32),
            pltpu.VMEM((STAGES, 2, comps * ny, nx), f32),
            pltpu.VMEM((STAGES, nz, nx), f32),
            pltpu.VMEM((STAGES, 2, comps, nz, nx), f32),
            pltpu.VMEM((STAGES, 2, comps * ny, nx), f32),
            pltpu.VMEM((STAGES, 2, nz, nx), f32),
            pltpu.VMEM((n_plane, share, ranks), f32),
            pltpu.VMEM((share, ranks), f32),
            pltpu.VMEM((n_plane, share, ranks), f32),
            pltpu.VMEM((n_gz, share, ranks), f32),
            pltpu.VMEM((n_plane, share, ranks), f32),
            pltpu.VMEM((1, ranks), f32),
            pltpu.VMEM((senders, 1, ranks), f32),
            pltpu.VMEM((1, ranks), f32),
            pltpu.VMEM((n_gz, 1, ranks), f32),
            dma((STAGES, 2)), dma((STAGES, 2)),
            dma((STAGES, 2)), dma((STAGES, 2)),
            dma((STAGES, 2)), dma((STAGES, 2)),
            dma((n_plane,)), dma((n_plane,)),
            dma((n_gz,)), dma((n_gz,)),
            dma((n_plane,)), dma((n_plane,)),
            dma((senders,)), dma((senders,)),
            dma((n_gz,)), dma((n_gz,)),
        ],
        compiler_params=pltpu.CompilerParams(
            collective_id=0, has_side_effects=True, vmem_limit_bytes=56 * 1024 * 1024
        ),
    )(velocity, strength, basis_old.reshape(modes, count, nx), snapshots.reshape(earlier_count, count, nx))
    field, level, basis_new = pl.pallas_call(
        rotate,
        out_shape=(
            jax.ShapeDtypeStruct(velocity.shape, f32),
            jax.ShapeDtypeStruct((ranks, ranks), f32),
            jax.ShapeDtypeStruct((ranks, count, nx), jnp.bfloat16),
        ),
        in_specs=[hbm] * 4,
        out_specs=(hbm,) * 3,
        scratch_shapes=[
            pltpu.VMEM(velocity.shape, f32),
            pltpu.VMEM((ranks, ranks), f32),
            pltpu.VMEM((ranks, ranks), jnp.bfloat16),
            pltpu.VMEM((ranks, length), jnp.bfloat16),
            pltpu.VMEM((ranks * count, nx), f32),
            pltpu.VMEM((ranks, count, nx), jnp.bfloat16),
            dma((4,)),
            dma((5,)),
            dma((4,)),
        ],
        compiler_params=pltpu.CompilerParams(vmem_limit_bytes=56 * 1024 * 1024),
    )(field, level, weights, whole)
    basis_new = basis_new.reshape(ranks, comps, ny // 2, nz // 2, nx)
    return (field, basis_new, level)


def solution(mesh):
    placed = (
        P(None, "gy", "gz", "grp"),
        P(None, None, "gy", "gz", "grp"),
        P(),
        P(None, None, "gy", "gz", "grp"),
    )
    return jax.shard_map(
        local,
        mesh=mesh,
        in_specs=placed,
        out_specs=(P(None, "gy", "gz", "grp"), P(None, None, "gy", "gz", "grp"), P()),
        check_vma=False,
    )
```

```python
import functools

import jax
import jax.numpy as jnp
from jax import lax
from jax.experimental import pallas as pl
from jax.experimental.pallas import tpu as pltpu
from jax.sharding import PartitionSpec as P

NS_ITERS = 8
STAGES = 6
DIRECT_LIMIT = 64
MESH = pl.DeviceIdType.MESH

time_step = 0.1
viscosity = 0.05


def each(count, body):
    if count <= 32:
        for i in range(count):
            body(i)
    else:
        lax.fori_loop(0, count, lambda i, carry: (body(i), carry)[1], 0)


def kernel(
    sizes, rows_total, v_hbm, strength_hbm, old_hbm, snap_hbm,
    field_hbm, level_ref, weights_ref, whole_hbm,
    field_ref, earlier_ref, store_sem,
    v_ref, strength_ref, old_ref, snap_ref, wide_ref, load_sem,
    rows_ref, stage, zsend, xsend, yrecv, zrecv, xrecv,
    gram_ref, part_ref, plane_ref, line_ref, full_ref,
    cross_send, cross_plane, cross_mid, cross_line,
    ysend_sem, yrecv_sem, zsend_sem, zrecv_sem, xsend_sem, xrecv_sem,
    asend_sem, arecv_sem, bsend_sem, brecv_sem, csend_sem, crecv_sem,
    dsend_sem, drecv_sem, esend_sem, erecv_sem,
):
    n_grp, n_gy, n_gz = sizes
    grp, gy, gz = lax.axis_index("grp"), lax.axis_index("gy"), lax.axis_index("gz")
    n_plane = n_grp * n_gy
    me = grp * n_gy + gy
    comps, ny, nz, nx = v_ref.shape
    ranks = earlier_ref.shape[0]
    lines = comps * ny

    def plane_id(offset):
        peer = lax.rem(me + offset, n_plane)
        return peer, {"grp": peer // n_gy, "gy": lax.rem(peer, n_gy)}

    everyone = n_plane * n_gz
    direct = everyone <= DIRECT_LIMIT
    my_place = me * n_gz + gz

    def any_id(offset):
        peer = lax.rem(my_place + offset, everyone)
        plane = peer // n_gz
        target = {"grp": plane // n_gy, "gy": lax.rem(plane, n_gy), "gz": lax.rem(peer, n_gz)}
        return peer, target

    def line_id(offset):
        peer = lax.rem(gz + offset, n_gz)
        return peer, {"gz": peer}

    y_up, y_down = {"gy": lax.rem(gy + 1, n_gy)}, {"gy": lax.rem(gy + n_gy - 1, n_gy)}
    z_up, z_down = {"gz": lax.rem(gz + 1, n_gz)}, {"gz": lax.rem(gz + n_gz - 1, n_gz)}
    x_up, x_down = {"grp": lax.rem(grp + 1, n_grp)}, {"grp": lax.rem(grp + n_grp - 1, n_grp)}
    x_ways = 1 if n_grp == 2 else 2

    loads = [
        pltpu.make_async_copy(v_hbm, v_ref, load_sem.at[2]),
        pltpu.make_async_copy(strength_hbm, strength_ref, load_sem.at[3]),
        pltpu.make_async_copy(old_hbm, old_ref, load_sem.at[0]),
        pltpu.make_async_copy(snap_hbm, snap_ref, load_sem.at[1]),
    ]
    for load in loads:
        load.start()
    barrier = pltpu.get_barrier_semaphore()

    def greet_plane(i):
        pl.semaphore_signal(barrier, inc=1, device_id=plane_id(i + 1)[1], device_id_type=MESH)

    def greet_line(i):
        pl.semaphore_signal(barrier, inc=1, device_id=line_id(i + 1)[1], device_id_type=MESH)

    def greet_any(i):
        pl.semaphore_signal(barrier, inc=1, device_id=any_id(i + 1)[1], device_id_type=MESH)

    if direct:
        each(everyone - 1, greet_any)
        greeted = everyone - 1
    else:
        each(n_plane - 1, greet_plane)
        each(n_gz - 1, greet_line)
        greeted = n_plane + n_gz - 2

    def remote(src, dst, send_sem, recv_sem, target):
        return pltpu.make_async_remote_copy(
            src_ref=src, dst_ref=dst, send_sem=send_sem, recv_sem=recv_sem,
            device_id=target, device_id_type=MESH,
        )

    def halo_copies(s):
        copies = [
            remote(stage.at[s, :, ny - 1], yrecv.at[s, 0], ysend_sem.at[s, 0], yrecv_sem.at[s, 0], y_up),
            remote(stage.at[s, :, 0], yrecv.at[s, 1], ysend_sem.at[s, 1], yrecv_sem.at[s, 1], y_down),
            remote(zsend.at[s, 0], zrecv.at[s, 0], zsend_sem.at[s, 0], zrecv_sem.at[s, 0], z_up),
            remote(zsend.at[s, 1], zrecv.at[s, 1], zsend_sem.at[s, 1], zrecv_sem.at[s, 1], z_down),
            remote(xsend.at[s], xrecv.at[s, 0], xsend_sem.at[s, 0], xrecv_sem.at[s, 0], x_up),
        ]
        if x_ways == 2:
            copies.append(
                remote(xsend.at[s], xrecv.at[s, 1], xsend_sem.at[s, 1], xrecv_sem.at[s, 1], x_down)
            )
        return copies

    lane = lax.broadcasted_iota(jnp.int32, (lines, nz, nx), 2)
    flat_lane = lax.broadcasted_iota(jnp.int32, (nz, nx), 1)
    pair = flat_lane // 2
    even = flat_lane % 2 == 0

    def send(s, f):
        copies = halo_copies(s)
        flat = f.reshape(lines, nz, nx)

        def pack_x():
            packed = jnp.zeros((nz, nx), jnp.float32)
            for k in range(lines):
                packed = jnp.where(pair == k, pltpu.roll(flat[k], 2 * k + 1, 1), packed)
            xsend[s] = packed

        rows_ref[0] = f.reshape(lines * nz, nx)
        zsend[s, 0] = rows_ref[0, pl.ds(nz - 1, lines, stride=nz), :]
        zsend[s, 1] = rows_ref[0, pl.ds(0, lines, stride=nz), :]
        if s == 0:
            stage[s] = f
            pack_x()
            pl.semaphore_wait(barrier, greeted)
        for copy in copies[2:4]:
            copy.start()
        if s > 0:
            stage[s] = f
        for copy in copies[:2]:
            copy.start()
        if s > 0:
            pack_x()
        for copy in copies[4:]:
            copy.start()
        return copies

    def stepped(s, f, copies):
        flat = f.reshape(lines, nz, nx)
        left, right = pltpu.roll(flat, 1, 2), pltpu.roll(flat, nx - 1, 2)
        rows_ref[1] = pltpu.roll(flat, 1, 1).reshape(lines * nz, nx)
        rows_ref[2] = pltpu.roll(flat, nz - 1, 1).reshape(lines * nz, nx)
        for copy in copies[:2]:
            copy.wait_recv()
        bottom = jnp.where(gy == 0, 0.0, yrecv[s, 0])
        upper = jnp.where(gy == n_gy - 1, 0.0, yrecv[s, 1])
        y_minus = jnp.concatenate([bottom[:, None], f[:, :-1]], axis=1)
        y_plus = jnp.concatenate([f[:, 1:], upper[:, None]], axis=1)
        carried = f[1][None] * (y_plus - y_minus) * 0.5
        spread = y_plus + y_minus - 6.0 * f
        for copy in copies[4:]:
            copy.wait_recv()
        from_left, from_right = xrecv[s, 0], xrecv[s, x_ways - 1]
        merged = jnp.where(even, from_left, pltpu.roll(from_right, nx - 2, 1))
        edges = jnp.stack([pltpu.roll(merged, (nx - 2 * k) % nx, 1) if k else merged for k in range(lines)])
        x_minus = jnp.where(lane == 0, edges, left).reshape(f.shape)
        x_plus = jnp.where(lane == nx - 1, edges, right).reshape(f.shape)
        carried = carried + f[0][None] * (x_plus - x_minus) * 0.5
        spread = spread + (x_plus + x_minus)
        for copy in copies[2:4]:
            copy.wait_recv()
        rows_ref[1, pl.ds(0, lines, stride=nz), :] = zrecv[s, 0]
        rows_ref[2, pl.ds(nz - 1, lines, stride=nz), :] = zrecv[s, 1]
        z_minus = rows_ref[1].reshape(f.shape)
        z_plus = rows_ref[2].reshape(f.shape)
        carried = carried + f[2][None] * (z_plus - z_minus) * 0.5
        spread = spread + (z_plus + z_minus)
        return f + time_step * (viscosity * spread - carried)

    def scatter_copy(i):
        peer, target = plane_id(i + 1)
        return remote(
            gram_ref.at[peer], plane_ref.at[me], asend_sem.at[i], arecv_sem.at[me], target
        )

    def line_copy(i):
        _, target = line_id(i + 1)
        return remote(part_ref, line_ref.at[gz], bsend_sem.at[i], brecv_sem.at[gz], target)

    def gather_copy(i):
        _, target = plane_id(i + 1)
        return remote(
            full_ref.at[me], full_ref.at[me], csend_sem.at[i], crecv_sem.at[me], target
        )

    def cross_plane_copy(i):
        _, target = plane_id(i + 1)
        return remote(cross_send, cross_plane.at[me], dsend_sem.at[i], drecv_sem.at[me], target)

    def cross_line_copy(i):
        _, target = line_id(i + 1)
        return remote(cross_mid, cross_line.at[gz], esend_sem.at[i], erecv_sem.at[gz], target)

    def cross_any_copy(i):
        _, target = any_id(i + 1)
        return remote(
            cross_send, cross_plane.at[my_place], dsend_sem.at[i], drecv_sem.at[my_place], target
        )

    def wait_any(buffer, sem):
        def body(i):
            peer, target = any_id(i + 1)
            remote(buffer.at[peer], buffer.at[peer], sem.at[peer], sem.at[peer], target).wait_recv()

        each(everyone - 1, body)

    def wait_plane(buffer, sem):
        def body(i):
            peer, target = plane_id(i + 1)
            remote(buffer.at[peer], buffer.at[peer], sem.at[peer], sem.at[peer], target).wait_recv()

        each(n_plane - 1, body)

    def wait_line(buffer, sem):
        def body(i):
            peer, target = line_id(i + 1)
            remote(buffer.at[peer], buffer.at[peer], sem.at[peer], sem.at[peer], target).wait_recv()

        each(n_gz - 1, body)

    modes, count = old_ref.shape[0], old_ref.shape[1]
    pitch = wide_ref.shape[0] // ranks

    def flatten_old():
        for load in loads[1:]:
            load.wait()

        def scale_row(r, carry):
            wide_ref[pl.ds(r * pitch, count), :] = strength_ref[r] * old_ref[r].astype(jnp.float32)
            return carry

        lax.fori_loop(0, modes, scale_row, 0, unroll=8)

    def flatten_snapshots():
        def copy_row(r, carry):
            wide_ref[pl.ds((r + modes) * pitch, count), :] = snap_ref[r].astype(jnp.float32)
            return carry

        lax.fori_loop(0, snap_ref.shape[0], copy_row, 0, unroll=7)
        wide_ref[pl.ds((ranks - 1) * pitch, count), :] = jnp.zeros((count, nx), jnp.float32)
        take_columns(0, count // 2)

    def take_columns(first, stop):
        for b in range(first, stop):
            column = wide_ref[pl.ds(b, ranks, stride=pitch), :]
            earlier_ref[:, b * nx : (b + 1) * nx] = column.astype(jnp.bfloat16)

    def begin_gram():
        take_columns(count // 2, count)
        earlier = earlier_ref[...]
        gram = lax.dot_general(
            earlier, earlier, (((1,), (1,)), ((), ())), preferred_element_type=jnp.float32
        )
        gram_ref[...] = gram.reshape(gram_ref.shape)
        plane_ref[me] = gram_ref[me]
        each(n_plane - 1, lambda i: scatter_copy(i).start())

    def add_plane():
        wait_plane(plane_ref, arecv_sem)
        part = jnp.sum(plane_ref[...], axis=0)
        part_ref[...] = part
        line_ref[gz] = part
        each(n_gz - 1, lambda i: line_copy(i).start())

    def add_line():
        wait_line(line_ref, brecv_sem)
        full_ref[me] = jnp.sum(line_ref[...], axis=0)
        each(n_plane - 1, lambda i: gather_copy(i).start())

    between = {0: flatten_old, 1: flatten_snapshots, 2: begin_gram, 3: add_plane, 4: add_line}
    loads[0].wait()
    base = v_ref[...]
    f = base
    for s in range(STAGES):
        copies = send(s, f)
        if s in between:
            between[s]()
        moved = stepped(s, f, copies)
        if s % 3 == 0:
            f = moved
        elif s % 3 == 1:
            f = 0.75 * base + 0.25 * moved
        else:
            f = base / 3.0 + 2.0 / 3.0 * moved
            base = f
    field_ref[...] = f
    field_store = pltpu.make_async_copy(field_ref, field_hbm, store_sem.at[0])
    field_store.start()

    blocks = [(c, y, z) for c in range(comps) for y in range(0, ny, 2) for z in range(0, nz, 2)]

    def newest_block(b):
        c, y, z = blocks[b]
        return field_ref[c, y, pl.ds(z, 1), :].astype(jnp.bfloat16).astype(jnp.float32)

    total = jnp.zeros((ranks, nx), jnp.float32)
    own = jnp.zeros((1, nx), jnp.float32)
    for b in range(len(blocks)):
        newest = newest_block(b)
        total = total + earlier_ref[:, b * nx : (b + 1) * nx].astype(jnp.float32) * newest
        own = own + newest * newest
    square_row = lax.broadcasted_iota(jnp.int32, (ranks, ranks), 0)
    square_col = lax.broadcasted_iota(jnp.int32, (ranks, ranks), 1)
    total = jnp.where(lax.broadcasted_iota(jnp.int32, (ranks, nx), 0) == ranks - 1, own, total)
    cross = jnp.sum(total.T, axis=0, keepdims=True)
    cross_send[...] = cross
    if direct:
        cross_plane[my_place] = cross
        each(everyone - 1, lambda i: cross_any_copy(i).start())
    else:
        cross_plane[me] = cross
        each(n_plane - 1, lambda i: cross_plane_copy(i).start())
    tail = slice(ranks - 16, ranks)
    last = lax.broadcasted_iota(jnp.int32, (16, nx), 0) == 15
    for b in range(len(blocks)):
        columns = slice(b * nx, (b + 1) * nx)
        rows = earlier_ref[tail, columns].astype(jnp.float32)
        earlier_ref[tail, columns] = jnp.where(last, newest_block(b), rows).astype(jnp.bfloat16)
    whole_store = pltpu.make_async_copy(earlier_ref, whole_hbm, store_sem.at[1])
    whole_store.start()
    wait_plane(full_ref, crecv_sem)
    if direct:
        wait_any(cross_plane, drecv_sem)
        cross = jnp.sum(cross_plane[...], axis=0)
    else:
        wait_plane(cross_plane, drecv_sem)
        cross_mid[...] = jnp.sum(cross_plane[...], axis=0)
        cross_line[gz] = cross_mid[...]
        each(n_gz - 1, lambda i: cross_line_copy(i).start())
        wait_line(cross_line, erecv_sem)
        cross = jnp.sum(cross_line[...], axis=0)
    cross = jnp.broadcast_to(cross, (ranks, ranks))

    gram = full_ref[...].reshape(ranks, ranks)
    gram = jnp.where(square_col == ranks - 1, cross.T, gram)
    gram = jnp.where(square_row == ranks - 1, cross, gram)
    scale = jnp.sqrt(jnp.sum(gram * gram, keepdims=True))
    level = gram / scale
    ident = jnp.where(square_row == square_col, 1.0, 0.0)

    def split(a):
        coarse = a.astype(jnp.bfloat16)
        return coarse, (a - coarse.astype(jnp.float32)).astype(jnp.bfloat16)

    def dot(left, right):
        terms = jnp.concatenate(right, axis=1)
        both = jnp.dot(
            jnp.concatenate(left, axis=1),
            jnp.concatenate([terms, terms], axis=0),
            preferred_element_type=jnp.float32,
        )
        return both[:, :ranks] + both[:, ranks:]

    inverse, inverse_split = ident, None
    for repeat in range(NS_ITERS):
        level_split = split(level)
        product = level if repeat == 0 else dot(inverse_split, level_split)
        product_split = split(product)
        moved = product if repeat == 0 else dot(product_split, inverse_split)
        inverse = 1.5 * inverse - 0.5 * moved
        level = 1.5 * level - 0.5 * dot(level_split, product_split)
        inverse_split = split(inverse)
    level_ref[...] = level
    factor = jnp.sqrt(jnp.full((1, 1), rows_total, jnp.float32)) / jnp.sqrt(scale)
    weights = (inverse * factor).astype(jnp.bfloat16)
    weights_ref[...] = weights

    field_store.wait()
    whole_store.wait()
    for s in range(STAGES):
        for copy in halo_copies(s):
            copy.wait_send()
    each(n_plane - 1, lambda i: scatter_copy(i).wait_send())
    each(n_gz - 1, lambda i: line_copy(i).wait_send())
    each(n_plane - 1, lambda i: gather_copy(i).wait_send())
    if direct:
        each(everyone - 1, lambda i: cross_any_copy(i).wait_send())
    else:
        each(n_plane - 1, lambda i: cross_plane_copy(i).wait_send())
        each(n_gz - 1, lambda i: cross_line_copy(i).wait_send())


def rotate(
    field_in, level_in, weights_in, whole_in, field_out, level_out, basis_out,
    field_ref, level_ref, weights_ref, whole_ref, wide_ref, basis_ref, pass_sem, load_sem, store_sem,
):
    ranks, count, nx = basis_ref.shape
    pitch = wide_ref.shape[0] // ranks
    parts = load_sem.shape[0] - 1
    width = count // parts * nx
    loads = [pltpu.make_async_copy(weights_in, weights_ref, load_sem.at[parts])]
    for p in range(parts):
        columns = (slice(None), pl.ds(p * width, width))
        loads.append(pltpu.make_async_copy(whole_in.at[columns], whole_ref.at[columns], load_sem.at[p]))
    arrivals = [
        pltpu.make_async_copy(field_in, field_ref, pass_sem.at[0]),
        pltpu.make_async_copy(level_in, level_ref, pass_sem.at[1]),
    ]
    passes = [
        pltpu.make_async_copy(field_ref, field_out, pass_sem.at[2]),
        pltpu.make_async_copy(level_ref, level_out, pass_sem.at[3]),
    ]
    for copy in loads + arrivals:
        copy.start()
    loads[0].wait()
    weights = weights_ref[...]
    for p in range(parts):
        loads[p + 1].wait()
        for b in range(p * count // parts, (p + 1) * count // parts, 2):
            pair = jnp.dot(
                weights, whole_ref[:, b * nx : (b + 2) * nx], preferred_element_type=jnp.float32
            )
            wide_ref[pl.ds(b, ranks, stride=pitch), :] = pair[:, :nx]
            wide_ref[pl.ds(b + 1, ranks, stride=pitch), :] = pair[:, nx:]
    for arrival, copy in zip(arrivals, passes):
        arrival.wait()
        copy.start()
    pieces = store_sem.shape[0]
    depth = ranks // pieces
    stores = []
    for p in range(pieces):
        rows = pl.ds(p * depth, depth)
        piece = wide_ref[pl.ds(p * depth * pitch, depth * pitch), :].reshape(depth, pitch, nx)
        basis_ref[rows] = piece[:, :count].astype(jnp.bfloat16)
        stores.append(pltpu.make_async_copy(basis_ref.at[rows], basis_out.at[rows], store_sem.at[p]))
        stores[-1].start()
    for copy in passes + stores:
        copy.wait()


def local(velocity, basis_old, strength, snapshots):
    modes = basis_old.shape[0]
    earlier_count = snapshots.shape[0]
    ranks = modes + earlier_count + 1
    sizes = tuple(lax.axis_size(axis) for axis in ("grp", "gy", "gz"))
    n_grp, n_gy, n_gz = sizes
    n_plane = n_grp * n_gy
    comps, ny, nz, nx = velocity.shape
    count = comps * (ny // 2) * (nz // 2)
    length = count * nx
    pitch = count + 8
    share = ranks // n_plane
    assert share * n_plane == ranks
    everyone = n_plane * n_gz
    senders = everyone if everyone <= DIRECT_LIMIT else n_plane
    f32 = jnp.float32
    dma = pltpu.SemaphoreType.DMA
    vmem = pl.BlockSpec(memory_space=pltpu.VMEM)
    hbm = pl.BlockSpec(memory_space=pltpu.HBM)
    field, level, weights, whole = pl.pallas_call(
        functools.partial(kernel, sizes, float(length * n_plane * n_gz)),
        out_shape=(
            jax.ShapeDtypeStruct(velocity.shape, f32),
            jax.ShapeDtypeStruct((ranks, ranks), f32),
            jax.ShapeDtypeStruct((ranks, ranks), jnp.bfloat16),
            jax.ShapeDtypeStruct((ranks, length), jnp.bfloat16),
        ),
        in_specs=[
            hbm,
            hbm,
            hbm,
            hbm,
        ],
        out_specs=(hbm, vmem, vmem, hbm),
        scratch_shapes=[
            pltpu.VMEM(velocity.shape, f32),
            pltpu.VMEM((ranks, length), jnp.bfloat16),
            dma((2,)),
            pltpu.VMEM(velocity.shape, f32),
            pltpu.SMEM((modes,), f32),
            pltpu.VMEM((modes, count, nx), jnp.bfloat16),
            pltpu.VMEM((earlier_count, count, nx), jnp.bfloat16),
            pltpu.VMEM((ranks * pitch, nx), f32),
            dma((4,)),
            pltpu.VMEM((3, comps * ny * nz, nx), f32),
            pltpu.VMEM((STAGES,) + velocity.shape, f32),
            pltpu.VMEM((STAGES, 2, comps * ny, nx), f32),
            pltpu.VMEM((STAGES, nz, nx), f32),
            pltpu.VMEM((STAGES, 2, comps, nz, nx), f32),
            pltpu.VMEM((STAGES, 2, comps * ny, nx), f32),
            pltpu.VMEM((STAGES, 2, nz, nx), f32),
            pltpu.VMEM((n_plane, share, ranks), f32),
            pltpu.VMEM((share, ranks), f32),
            pltpu.VMEM((n_plane, share, ranks), f32),
            pltpu.VMEM((n_gz, share, ranks), f32),
            pltpu.VMEM((n_plane, share, ranks), f32),
            pltpu.VMEM((1, ranks), f32),
            pltpu.VMEM((senders, 1, ranks), f32),
            pltpu.VMEM((1, ranks), f32),
            pltpu.VMEM((n_gz, 1, ranks), f32),
            dma((STAGES, 2)), dma((STAGES, 2)),
            dma((STAGES, 2)), dma((STAGES, 2)),
            dma((STAGES, 2)), dma((STAGES, 2)),
            dma((n_plane,)), dma((n_plane,)),
            dma((n_gz,)), dma((n_gz,)),
            dma((n_plane,)), dma((n_plane,)),
            dma((senders,)), dma((senders,)),
            dma((n_gz,)), dma((n_gz,)),
        ],
        compiler_params=pltpu.CompilerParams(
            collective_id=0, has_side_effects=True, vmem_limit_bytes=56 * 1024 * 1024
        ),
    )(velocity, strength, basis_old.reshape(modes, count, nx), snapshots.reshape(earlier_count, count, nx))
    field, level, basis_new = pl.pallas_call(
        rotate,
        out_shape=(
            jax.ShapeDtypeStruct(velocity.shape, f32),
            jax.ShapeDtypeStruct((ranks, ranks), f32),
            jax.ShapeDtypeStruct((ranks, count, nx), jnp.bfloat16),
        ),
        in_specs=[hbm] * 4,
        out_specs=(hbm,) * 3,
        scratch_shapes=[
            pltpu.VMEM(velocity.shape, f32),
            pltpu.VMEM((ranks, ranks), f32),
            pltpu.VMEM((ranks, ranks), jnp.bfloat16),
            pltpu.VMEM((ranks, length), jnp.bfloat16),
            pltpu.VMEM((ranks * pitch, nx), f32),
            pltpu.VMEM((ranks, count, nx), jnp.bfloat16),
            dma((4,)),
            dma((5,)),
            dma((4,)),
        ],
        compiler_params=pltpu.CompilerParams(vmem_limit_bytes=56 * 1024 * 1024),
    )(field, level, weights, whole)
    basis_new = basis_new.reshape(ranks, comps, ny // 2, nz // 2, nx)
    return (field, basis_new, level)


def solution(mesh):
    placed = (
        P(None, "gy", "gz", "grp"),
        P(None, None, "gy", "gz", "grp"),
        P(),
        P(None, None, "gy", "gz", "grp"),
    )
    return jax.shard_map(
        local,
        mesh=mesh,
        in_specs=placed,
        out_specs=(P(None, "gy", "gz", "grp"), P(None, None, "gy", "gz", "grp"), P()),
        check_vma=False,
    )
```
